32 devices in a mesh: groups: 2 (over y), shard: 4 (over z), qgrp: 2 (over x), dim: 2 (over core).
Axes of the slice: x: 2, y: 2, z: 4, core: 2. Of those that a mesh axis runs over, the one named last changes fastest.
Arguments:
- queries: bfloat16 [32, 32, 128], P(('groups', 'shard', 'qgrp')), parts along dimension 0, may hold values from -0.5 to 0.5
- doc_tokens: bfloat16 [512, 128, 128], P(('groups', 'shard', 'qgrp'), 'dim'), parts along dimension 0, may hold values from -0.5 to 0.5
- doc_lens: int32 [512], P(('groups', 'shard', 'qgrp')), parts along dimension 0, may hold values from 1 to 128
- candidates: int32 [32, 1000], P(('groups', 'shard', 'qgrp')), parts along dimension 0, may hold values from 0 to 255
Outputs:
- scores: float32 [32, 1000], P(('groups', 'shard', 'qgrp')), parts along dimension 0
The draws below stay inside these ranges and needn't reach their ends.
There are 2 independent parts, one for each index of `groups`. The reference program is written for one: setup_inputs(seed, part) draws one part's arguments, and reference() takes and returns one part's arrays. A program takes and returns all parts, laid end to end along the dimension named above; each array names one. Nothing has to cross between parts.
All inputs are finite; a program needn't handle non-finite values.
Results may differ from the reference program's by a relative error of at most 0.0003.
Values may be sent and summed in bfloat16 or wider, within the bound.
No kernel may reach another device: no remote copies, remote signals or barrier semaphores. Data moves between devices by JAX's collectives and lax.ppermute only.
A program may use at most 64 MiB of HBM per device.

```python
import jax
import jax.numpy as jnp
from jax import lax

DIM = 128
QTOK = 32
LTOK = 128
CAND = 1000
QUERIES = 16
PASSAGES = 256


def touch_ends(values, own_key, least, top_value):
    spot = [jax.random.randint(jax.random.fold_in(own_key, axis), (), 0, length) for axis, length in enumerate(values.shape)]
    main_axis = values.shape.index(max(values.shape))
    next_to = spot[:main_axis] + [(spot[main_axis] + 1) % values.shape[main_axis]] + spot[main_axis + 1:]
    return values.at[tuple(spot)].set(least).at[tuple(next_to)].set(top_value)


def block_scale(rng, dims, cuts, smallest, high):
    loudness = 1.0
    for position, parts in cuts:
        heights = jax.random.uniform(jax.random.fold_in(jax.random.fold_in(rng, 6), position), (parts,), jnp.float32, smallest / len(cuts), high / len(cuts))
        loudness = loudness * jnp.repeat(jnp.exp(heights), dims[position] // parts).reshape((-1,) + (1,) * (len(dims) - 1 - position))
    return loudness


def bell_draw(key, dims, scale, reach, shards=(), kind=jnp.bfloat16):
    result = jax.random.normal(key, dims, jnp.float32) * scale
    if len(shards) > 0:
        result = block_scale(key, dims, shards, -0.22, 0.18) * result
    return jnp.clip(result, min=-reach, max=reach).astype(kind)


def setup_inputs(seed: int = 0, part: int = 0) -> dict:
    keys = jax.random.split(jax.random.key(seed), 5)
    part_keys = jax.random.split(jax.random.fold_in(keys[4], part), 5)
    queries = bell_draw(part_keys[0], (QUERIES, QTOK, DIM), DIM ** -0.5, 0.5, ((0, 8),))
    doc_tokens = bell_draw(part_keys[1], (PASSAGES, LTOK, DIM), DIM ** -0.5, 0.5, ((0, 8), (1, 2)))
    doc_lens = touch_ends(jax.random.randint(part_keys[2], (PASSAGES,), 1, LTOK + 1), jax.random.fold_in(part_keys[2], 1), 1, LTOK).astype(jnp.int32)
    candidates = touch_ends(jax.random.randint(part_keys[3], (QUERIES, CAND), 0, PASSAGES), jax.random.fold_in(part_keys[3], 1), 0, PASSAGES - 1).astype(jnp.int32)
    return dict(queries=queries, doc_tokens=doc_tokens, doc_lens=doc_lens, candidates=candidates)


def reference(queries, doc_tokens, doc_lens, candidates):
    flat_queries = queries.reshape(QUERIES * QTOK, DIM)
    tiles = doc_tokens.reshape(PASSAGES // 8, 8 * LTOK, DIM)
    positions = jnp.arange(LTOK, dtype=jnp.int32)
    valid = (positions[None, :] < doc_lens[:, None]).reshape(PASSAGES // 8, 8 * LTOK)

    def one_tile(pair):
        tile, mask = pair
        token_score = jnp.dot(flat_queries, tile.T, preferred_element_type=jnp.float32)
        token_score = jnp.where(mask[None, :], token_score, jnp.float32(-1e30))
        return jnp.max(token_score.reshape(QUERIES * QTOK, 8, LTOK), axis=2)

    token_max = lax.map(one_tile, (tiles, valid))
    token_max = jnp.transpose(token_max, (1, 0, 2)).reshape(QUERIES, QTOK, PASSAGES)
    passage_score = jnp.sum(token_max, axis=1)
    return jnp.take_along_axis(passage_score, candidates, axis=1)
```

```python
import functools

import jax
import jax.numpy as jnp
from jax import lax
from jax.experimental import pallas as pl
from jax.experimental.pallas import tpu as pltpu
from jax.sharding import PartitionSpec as P

INDEX_AXES = ("shard", "qgrp")
LOW = -1e30
STEP = 4
DIRECT = 16


def score_kernel(n_own, count, me_ref, lens_ref, *refs):
    piece_refs = refs[: n_own]
    own_ref, other_ref = refs[n_own: n_own + 2]
    out_refs = refs[n_own + 2: -2]
    flat_ref, max_ref = refs[-2:]
    core = me_ref[0]
    at = 0
    for piece_ref in piece_refs:
        rows, q_tokens, width = piece_ref.shape
        flat_ref[pl.ds(at, rows * q_tokens), :] = piece_ref[...].reshape(rows * q_tokens, width)
        at += rows * q_tokens
    half = own_ref.shape[1]
    q_tokens = piece_refs[0].shape[1]
    total = flat_ref.shape[0]
    rows = lax.broadcasted_iota(jnp.int32, (half, 1), 0)
    block = 512 if total % 512 == 0 else total

    def group(step, _):
        start = step * STEP
        for at in range(0, total, block):
            flat = flat_ref[pl.ds(at, block), :]
            for k in range(STEP):
                p = start + k
                length = lens_ref[p]
                best = None
                for ref, offset in ((own_ref, core * half), (other_ref, (1 - core) * half)):
                    score = lax.dot_general(
                        ref[p], flat, (((1,), (1,)), ((), ())), preferred_element_type=jnp.float32
                    )
                    score = jnp.where(rows + offset < length, score, LOW)
                    best = score if best is None else jnp.maximum(best, score)
                max_ref[pl.ds(p, 1), pl.ds(at, block)] = jnp.max(best, axis=0, keepdims=True)
        return 0

    lax.fori_loop(0, count // STEP, group, 0)
    queries = total // q_tokens
    summed = jnp.sum(max_ref[...].T.reshape(queries, q_tokens, count), axis=1)
    q_each = out_refs[0].shape[0]
    if len(out_refs) == 1:
        out_refs[0][...] = summed
    else:
        for r, out_ref in enumerate(out_refs):
            out_ref[...] = summed[r * q_each: (r + 1) * q_each]


def pick_kernel(n_own, base_ref, cand_ref, *refs):
    piece_refs, out_ref = refs[:n_own], refs[n_own]
    parts = [ref[...] for ref in piece_refs]
    table = jnp.concatenate(parts, axis=1) if len(parts) > 1 else parts[0]
    size = table.shape[1]
    spot = cand_ref[...] - base_ref[0]
    spot = jnp.where(spot < 0, spot + size, spot)
    rows, width = spot.shape
    lane_count = 128
    for at in range(0, width, lane_count):
        index = spot[:, at: at + lane_count]
        low = jnp.bitwise_and(index, lane_count - 1)
        high = lax.shift_right_logical(index, 7)
        value = jnp.zeros((rows, lane_count), jnp.float32)
        for t in range(0, size, lane_count):
            found = jnp.take_along_axis(table[:, t: t + lane_count], low, axis=1, mode="promise_in_bounds")
            value = jnp.where(high == t // lane_count, found, value)
        out_ref[:, pl.ds(at, lane_count)] = value


def per_device(queries, doc_tokens, doc_lens, candidates):
    q_owned, cand = candidates.shape
    n = lax.axis_size("shard") * lax.axis_size("qgrp")
    cores = lax.axis_size("dim")
    _, q_tokens, width = queries.shape
    count = doc_tokens.shape[0]
    me = lax.axis_index(INDEX_AXES)
    core = lax.axis_index("dim")
    direct = n <= DIRECT

    def turn(x, r):
        return lax.ppermute(x, INDEX_AXES, [(s, (s + r) % n) for s in range(n)])

    if direct:
        pieces = [queries] + [turn(queries, n - r) for r in range(1, n)]
    else:
        pieces = [lax.all_gather(queries, INDEX_AXES, axis=0, tiled=True)]
    other = lax.ppermute(doc_tokens, "dim", [(s, cores - 1 - s) for s in range(cores)])

    smem = pl.BlockSpec(memory_space=pltpu.SMEM)
    vmem = pl.BlockSpec(memory_space=pltpu.VMEM)
    outs = n if direct else 1
    blocks = pl.pallas_call(
        functools.partial(score_kernel, len(pieces), count),
        out_shape=[jax.ShapeDtypeStruct((n * q_owned // outs, count), jnp.float32)] * outs,
        in_specs=[smem, smem] + [vmem] * (len(pieces) + 2),
        out_specs=[vmem] * outs,
        scratch_shapes=[
            pltpu.VMEM((n * q_owned * q_tokens, width), jnp.bfloat16),
            pltpu.VMEM((count, n * q_owned * q_tokens), jnp.float32),
        ],
        compiler_params=pltpu.CompilerParams(vmem_limit_bytes=48 * 1024 * 1024),
        name="score",
    )(core.reshape(1), doc_lens, *pieces, doc_tokens, other)

    if direct:
        moved = [blocks[0]] + [turn(blocks[r], r) for r in range(1, n)]
        moved = [moved[0]] + [moved[n - r] for r in range(1, n)]
        base = me * count
    else:
        moved = [
            lax.all_to_all(
                blocks[0].reshape(n, q_owned, count), INDEX_AXES, split_axis=0, concat_axis=0, tiled=True
            ).transpose(1, 0, 2).reshape(q_owned, n * count)
        ]
        base = jnp.zeros((), jnp.int32)
    padded = -(-cand // 128) * 128
    return pl.pallas_call(
        functools.partial(pick_kernel, len(moved)),
        grid=(1,),
        out_shape=jax.ShapeDtypeStruct((q_owned, cand), jnp.float32),
        in_specs=[smem, pl.BlockSpec((q_owned, padded), lambda i: (0, 0))]
        + [pl.BlockSpec(m.shape, lambda i: (0, 0)) for m in moved],
        out_specs=pl.BlockSpec((q_owned, padded), lambda i: (0, 0)),
        name="pick",
    )(base.reshape(1), candidates, *moved)


def solution(mesh):
    in_specs = (
        P(("groups",) + INDEX_AXES, None, None),
        P(("groups",) + INDEX_AXES, "dim", None),
        P(("groups",) + INDEX_AXES),
        P(("groups",) + INDEX_AXES, None),
    )
    out_specs = P(("groups",) + INDEX_AXES, None)
    return jax.shard_map(
        per_device, mesh=mesh, in_specs=in_specs, out_specs=out_specs, check_vma=False
    )
```

```python
import functools

import jax
import jax.numpy as jnp
from jax import lax
from jax.experimental import pallas as pl
from jax.experimental.pallas import tpu as pltpu
from jax.sharding import PartitionSpec as P

INDEX_AXES = ("shard", "qgrp")
ALL_AXES = ("shard", "qgrp", "dim")
LOW = -1e30
LANES = 128
BLOCK = 256


def bits_of(size):
    return size.bit_length() - 1


def score_kernel(n_pieces, me_ref, lens_ref, *refs):
    piece_refs = refs[:n_pieces]
    own_ref, other_ref = refs[n_pieces: n_pieces + 2]
    out_refs = refs[n_pieces + 2: -2]
    flat_ref, max_ref = refs[-2:]
    core = me_ref[0]
    q_tokens, width = piece_refs[0].shape[1:]
    count, half, _ = own_ref.shape
    total = flat_ref.shape[0]
    firsts = n_pieces - len(out_refs) + 1
    at = 0
    for k in range(firsts - 1, n_pieces):
        rows = piece_refs[k].shape[0] * q_tokens
        piece = piece_refs[k][...].reshape(rows, width)
        if k == firsts - 1 and firsts == 2:
            piece = jnp.where(core == 0, piece_refs[0][...].reshape(rows, width), piece)
        flat_ref[pl.ds(at, rows), :] = piece
        at += rows
    block = min(total, BLOCK)
    step = min(count, 8)
    rows = lax.broadcasted_iota(jnp.int32, (half, block), 0)
    own_at = core * half

    def group(g, _):
        start = g * step
        for at in range(0, total, block):
            flat = flat_ref[pl.ds(at, block), :]
            scores = []
            for ref in (own_ref, other_ref):
                docs = ref[pl.ds(start, step)].reshape(step * half, width)
                scores.append(lax.dot_general(
                    docs, flat, (((1,), (1,)), ((), ())), preferred_element_type=jnp.float32
                ))
            for k in range(step):
                length = lens_ref[start + k]
                one = jnp.where(rows < length - own_at, scores[0][k * half: (k + 1) * half], LOW)
                two = jnp.where(rows < length - (half - own_at), scores[1][k * half: (k + 1) * half], LOW)
                best = jnp.max(jnp.maximum(one, two), axis=0, keepdims=True)
                max_ref[pl.ds(start + k, 1), pl.ds(at, block)] = best
        return 0

    lax.fori_loop(0, count // step, group, 0)
    summed = jnp.sum(max_ref[...].T.reshape(total // q_tokens, q_tokens, count), axis=1)
    q_each = out_refs[0].shape[0]
    for r, out_ref in enumerate(out_refs):
        out_ref[...] = summed[r * q_each: (r + 1) * q_each]


def score(core, doc_lens, pieces, doc_tokens, other, outs):
    smem = pl.BlockSpec(memory_space=pltpu.SMEM)
    vmem = pl.BlockSpec(memory_space=pltpu.VMEM)
    count = doc_tokens.shape[0]
    used = pieces if len(pieces) <= outs else pieces[1:]
    queries = sum(p.shape[0] for p in used)
    q_tokens, width = pieces[0].shape[1:]
    return pl.pallas_call(
        functools.partial(score_kernel, len(pieces)),
        out_shape=[jax.ShapeDtypeStruct((queries // outs, count), jnp.float32)] * outs,
        in_specs=[smem, smem] + [vmem] * (len(pieces) + 2),
        out_specs=[vmem] * outs,
        scratch_shapes=[
            pltpu.VMEM((queries * q_tokens, width), jnp.bfloat16),
            pltpu.VMEM((count, queries * q_tokens), jnp.float32),
        ],
        compiler_params=pltpu.CompilerParams(vmem_limit_bytes=24 * 1024 * 1024),
        name="score",
    )(core.reshape(1), doc_lens, *pieces, doc_tokens, other)


def pick_kernel(n_pieces, place, where_ref, cand_ref, *refs):
    piece_refs, out_ref = refs[:n_pieces], refs[n_pieces]
    parts = [ref[...] for ref in piece_refs]
    table = jnp.concatenate(parts, axis=1) if len(parts) > 1 else parts[0]
    size = table.shape[1]
    cand = cand_ref[...]
    rows, width = cand.shape
    spot = place(cand, where_ref)
    for at in range(0, width, LANES):
        wide = min(LANES, width - at)
        index = spot[:, at: at + wide]
        if wide < LANES:
            index = jnp.concatenate([index, jnp.zeros((rows, LANES - wide), jnp.int32)], axis=1)
        low = jnp.bitwise_and(index, LANES - 1)
        high = lax.shift_right_logical(index, bits_of(LANES))
        value = jnp.zeros((rows, LANES), jnp.float32)
        for t in range(0, size, LANES):
            found = jnp.take_along_axis(table[:, t: t + LANES], low, axis=1, mode="promise_in_bounds")
            value = jnp.where(high == t // LANES, found, value)
        out_ref[:, pl.ds(at, wide)] = value[:, :wide]


def pick(place, where, candidates, pieces):
    smem = pl.BlockSpec(memory_space=pltpu.SMEM)
    vmem = pl.BlockSpec(memory_space=pltpu.VMEM)
    return pl.pallas_call(
        functools.partial(pick_kernel, len(pieces), place),
        out_shape=jax.ShapeDtypeStruct(candidates.shape, jnp.float32),
        in_specs=[smem, vmem] + [vmem] * len(pieces),
        out_specs=vmem,
        name="pick",
    )(where, candidates, *pieces)


def two_columns(queries, doc_tokens, other, doc_lens, candidates, n_z, core):
    count = doc_tokens.shape[0]

    def flat(z, x, d):
        return ((z % n_z) * 2 + x) * 2 + d

    def to_scorer(array, r):
        pairs = [(flat(z + r, x ^ d, d), flat(z, x, d)) for z in range(n_z) for x in range(2) for d in range(2)]
        return lax.ppermute(array, ALL_AXES, [pair for pair in pairs if pair[0] != pair[1]])

    def to_owner(array, r):
        pairs = [(flat(z, x, d), flat(z + r, x ^ d, d)) for z in range(n_z) for x in range(2) for d in range(2)]
        return lax.ppermute(array, ALL_AXES, [pair for pair in pairs if pair[0] != pair[1]])

    def to_core(array):
        return lax.ppermute(array, "dim", [(0, 1), (1, 0)])

    pieces = [queries] + [to_scorer(queries, r) for r in range(n_z)]
    blocks = score(core, doc_lens, pieces, doc_tokens, other, n_z)
    moved = [to_owner(block, r) for r, block in enumerate(blocks)]
    moved[0] = jnp.where(core == 0, blocks[0], moved[0])
    crossed = [to_core(block) for block in moved]

    def place(cand, where_ref):
        p = jnp.bitwise_and(cand, count - 1)
        chip = lax.shift_right_logical(cand, bits_of(count))
        r = jnp.bitwise_and(where_ref[0] - lax.shift_right_logical(chip, 1), n_z - 1)
        side = jnp.bitwise_and(jnp.bitwise_xor(chip, where_ref[1]), 1)
        return (side * n_z + r) * count + p

    where = jnp.stack([lax.axis_index("shard"), lax.axis_index("qgrp") ^ core])
    return pick(place, where, candidates, moved + crossed)


def any_columns(queries, doc_tokens, other, doc_lens, candidates, n, core):
    q_owned = candidates.shape[0]
    count = doc_tokens.shape[0]
    gathered = lax.all_gather(queries, INDEX_AXES, axis=0, tiled=True)
    block = score(core, doc_lens, [gathered], doc_tokens, other, 1)[0]
    moved = lax.all_to_all(
        block.reshape(n, q_owned, count), INDEX_AXES, split_axis=0, concat_axis=0, tiled=True
    )
    table = moved.transpose(1, 0, 2).reshape(q_owned, n * count)
    return pick(lambda cand, where_ref: cand, jnp.zeros((1,), jnp.int32), candidates, [table])


def per_device(queries, doc_tokens, doc_lens, candidates):
    n_z, n_x, cores = (lax.axis_size(axis) for axis in ALL_AXES)
    count = doc_tokens.shape[0]
    core = lax.axis_index("dim")
    other = lax.ppermute(doc_tokens, "dim", [(s, cores - 1 - s) for s in range(cores)])
    power = count & (count - 1) == 0 and n_z & (n_z - 1) == 0
    if n_x == 2 and cores == 2 and n_z <= 8 and power:
        return two_columns(queries, doc_tokens, other, doc_lens, candidates, n_z, core)
    return any_columns(queries, doc_tokens, other, doc_lens, candidates, n_z * n_x, core)


def solution(mesh):
    in_specs = (
        P(("groups",) + INDEX_AXES, None, None),
        P(("groups",) + INDEX_AXES, "dim", None),
        P(("groups",) + INDEX_AXES),
        P(("groups",) + INDEX_AXES, None),
    )
    out_specs = P(("groups",) + INDEX_AXES, None)
    return jax.shard_map(
        per_device, mesh=mesh, in_specs=in_specs, out_specs=out_specs, check_vma=False
    )
```

```python
import functools

import jax
import jax.numpy as jnp
from jax import lax
from jax.experimental import pallas as pl
from jax.experimental.pallas import tpu as pltpu
from jax.sharding import PartitionSpec as P

INDEX_AXES = ("shard", "qgrp")
ALL_AXES = ("shard", "qgrp", "dim")
LOW = -1e30
LANES = 128
BLOCK = 256


def score_kernel(n_pieces, me_ref, lens_ref, *refs):
    piece_refs = refs[:n_pieces]
    own_ref, other_ref = refs[n_pieces: n_pieces + 2]
    out_refs = refs[n_pieces + 2: -4]
    flat_ref, max_ref, held_ref, sem = refs[-4:]
    core = me_ref[0]
    q_tokens, width = piece_refs[0].shape[1:]
    count, half, _ = own_ref.shape
    total = flat_ref.shape[0]
    fetch = pltpu.make_async_copy(own_ref, held_ref, sem)
    fetch.start()
    at = 0
    for piece_ref in piece_refs:
        rows = piece_ref.shape[0] * q_tokens
        flat_ref[pl.ds(at, rows), :] = piece_ref[...].reshape(rows, width)
        at += rows
    block = min(total, BLOCK)
    step = min(count, 8)
    rows = lax.broadcasted_iota(jnp.int32, (half, block), 0)

    def best_of(ref, first, fold):
        def group(g, _):
            start = g * step
            docs = ref[pl.ds(start, step)].reshape(step * half, width)
            for at in range(0, total, block):
                flat = flat_ref[pl.ds(at, block), :]
                scores = lax.dot_general(
                    docs, flat, (((1,), (1,)), ((), ())), preferred_element_type=jnp.float32
                )
                for k in range(step):
                    part = scores[k * half: (k + 1) * half]
                    part = jnp.where(rows < lens_ref[start + k] - first, part, LOW)
                    best = jnp.max(part, axis=0, keepdims=True)
                    spot = pl.ds(start + k, 1), pl.ds(at, block)
                    max_ref[spot] = jnp.maximum(max_ref[spot], best) if fold else best
            return 0

        lax.fori_loop(0, count // step, group, 0)

    best_of(other_ref, (1 - core) * half, False)
    fetch.wait()
    best_of(held_ref, core * half, True)
    summed = jnp.sum(max_ref[...].T.reshape(total // q_tokens, q_tokens, count), axis=1)
    q_each = out_refs[0].shape[0]
    for r, out_ref in enumerate(out_refs):
        out_ref[...] = summed[r * q_each: (r + 1) * q_each]


def score(core, doc_lens, pieces, doc_tokens, other, outs):
    smem = pl.BlockSpec(memory_space=pltpu.SMEM)
    vmem = pl.BlockSpec(memory_space=pltpu.VMEM)
    hbm = pl.BlockSpec(memory_space=pltpu.HBM)
    count = doc_tokens.shape[0]
    queries = sum(p.shape[0] for p in pieces)
    q_tokens, width = pieces[0].shape[1:]
    return pl.pallas_call(
        functools.partial(score_kernel, len(pieces)),
        out_shape=[jax.ShapeDtypeStruct((queries // outs, count), jnp.float32)] * outs,
        in_specs=[smem, smem] + [vmem] * len(pieces) + [hbm, vmem],
        out_specs=[vmem] * outs,
        scratch_shapes=[
            pltpu.VMEM((queries * q_tokens, width), jnp.bfloat16),
            pltpu.VMEM((count, queries * q_tokens), jnp.float32),
            pltpu.VMEM(doc_tokens.shape, jnp.bfloat16),
            pltpu.SemaphoreType.DMA(()),
        ],
        compiler_params=pltpu.CompilerParams(vmem_limit_bytes=(8 + queries // 16) * 1024 * 1024),
        name="score",
    )(core.reshape(1), doc_lens, *pieces, doc_tokens, other)


def pick_kernel(n_pieces, base_ref, cand_ref, *refs):
    piece_refs, out_ref = refs[:n_pieces], refs[n_pieces]
    parts = [ref[...] for ref in piece_refs]
    table = jnp.concatenate(parts, axis=1) if len(parts) > 1 else parts[0]
    size = table.shape[1]
    rows, width = cand_ref.shape
    spot = jnp.bitwise_xor(cand_ref[...], base_ref[0])
    for at in range(0, width, LANES):
        wide = min(LANES, width - at)
        index = spot[:, at: at + wide]
        if wide < LANES:
            index = jnp.concatenate([index, jnp.zeros((rows, LANES - wide), jnp.int32)], axis=1)
        low = jnp.bitwise_and(index, LANES - 1)
        high = lax.shift_right_logical(index, LANES.bit_length() - 1)
        value = jnp.zeros((rows, LANES), jnp.float32)
        for t in range(0, size, LANES):
            found = jnp.take_along_axis(table[:, t: t + LANES], low, axis=1, mode="promise_in_bounds")
            value = jnp.where(high == t // LANES, found, value)
        out_ref[:, pl.ds(at, wide)] = value[:, :wide]


def pick(base, candidates, pieces):
    smem = pl.BlockSpec(memory_space=pltpu.SMEM)
    vmem = pl.BlockSpec(memory_space=pltpu.VMEM)
    return pl.pallas_call(
        functools.partial(pick_kernel, len(pieces)),
        out_shape=jax.ShapeDtypeStruct(candidates.shape, jnp.float32),
        in_specs=[smem, vmem] + [vmem] * len(pieces),
        out_specs=vmem,
        compiler_params=pltpu.CompilerParams(vmem_limit_bytes=4 * 1024 * 1024),
        name="pick",
    )(base.reshape(1), candidates, *pieces)


def two_columns(queries, doc_tokens, other, doc_lens, candidates, n_z, core):
    count = doc_tokens.shape[0]

    def exchange(array, r):
        pairs = [
            ((z * 2 + x) * 2 + d, ((z ^ r) * 2 + (x ^ d)) * 2 + d)
            for z in range(n_z) for x in range(2) for d in range(2)
        ]
        return lax.ppermute(array, ALL_AXES, pairs)

    pieces = [exchange(queries, r) for r in range(n_z)]
    blocks = score(core, doc_lens, pieces, doc_tokens, other, n_z)
    table = []
    for r in range(n_z):
        moved = exchange(blocks[r], r)
        table += [moved, lax.ppermute(moved, "dim", [(0, 1), (1, 0)])]
    base = (lax.axis_index("shard") * 2 + (lax.axis_index("qgrp") ^ core)) * count
    return pick(base, candidates, table)


def any_columns(queries, doc_tokens, other, doc_lens, candidates, n, core):
    q_owned = candidates.shape[0]
    count = doc_tokens.shape[0]
    gathered = lax.all_gather(queries, INDEX_AXES, axis=0, tiled=True)
    block = score(core, doc_lens, [gathered], doc_tokens, other, 1)[0]
    moved = lax.all_to_all(
        block.reshape(n, q_owned, count), INDEX_AXES, split_axis=0, concat_axis=0, tiled=True
    )
    table = moved.transpose(1, 0, 2).reshape(q_owned, n * count)
    return pick(jnp.int32(0), candidates, [table])


def per_device(queries, doc_tokens, doc_lens, candidates):
    n_z, n_x, cores = (lax.axis_size(axis) for axis in ALL_AXES)
    count = doc_tokens.shape[0]
    core = lax.axis_index("dim")
    other = lax.ppermute(doc_tokens, "dim", [(s, cores - 1 - s) for s in range(cores)])
    power = count & (count - 1) == 0 and n_z & (n_z - 1) == 0
    if n_x == 2 and cores == 2 and n_z <= 8 and power:
        return two_columns(queries, doc_tokens, other, doc_lens, candidates, n_z, core)
    return any_columns(queries, doc_tokens, other, doc_lens, candidates, n_z * n_x, core)


def solution(mesh):
    in_specs = (
        P(("groups",) + INDEX_AXES, None, None),
        P(("groups",) + INDEX_AXES, "dim", None),
        P(("groups",) + INDEX_AXES),
        P(("groups",) + INDEX_AXES, None),
    )
    out_specs = P(("groups",) + INDEX_AXES, None)
    return jax.shard_map(
        per_device, mesh=mesh, in_specs=in_specs, out_specs=out_specs, check_vma=False
    )
```

```python
import functools

import jax
import jax.numpy as jnp
from jax import lax
from jax.experimental import pallas as pl
from jax.experimental.pallas import tpu as pltpu
from jax.sharding import PartitionSpec as P

INDEX_AXES = ("shard", "qgrp")
ALL_AXES = ("shard", "qgrp", "dim")
LOW = -1e30
LANES = 128
BLOCK = 256


def score_kernel(n_pieces, put, me_ref, lens_ref, *refs):
    piece_refs = refs[:n_pieces]
    own_ref, other_ref = refs[n_pieces: n_pieces + 2]
    out_refs = refs[n_pieces + 2: -4]
    flat_ref, max_ref, held_ref, sem = refs[-4:]
    core = me_ref[0]
    q_tokens, width = piece_refs[0].shape[1:]
    count, half, _ = own_ref.shape
    total = flat_ref.shape[0]
    fetch = pltpu.make_async_copy(own_ref, held_ref, sem)
    fetch.start()
    at = 0
    for piece_ref in piece_refs:
        rows = piece_ref.shape[0] * q_tokens
        flat_ref[pl.ds(at, rows), :] = piece_ref[...].reshape(rows, width)
        at += rows
    block = min(total, BLOCK)
    step = min(count, 8)
    rows = lax.broadcasted_iota(jnp.int32, (half, block), 0)

    def best_of(ref, first, fold):
        def group(g, _):
            start = g * step
            docs = ref[pl.ds(start, step)].reshape(step * half, width)
            for at in range(0, total, block):
                flat = flat_ref[pl.ds(at, block), :]
                scores = lax.dot_general(
                    docs, flat, (((1,), (1,)), ((), ())), preferred_element_type=jnp.float32
                )
                for k in range(step):
                    part = scores[k * half: (k + 1) * half]
                    part = jnp.where(rows < lens_ref[start + k] - first, part, LOW)
                    best = jnp.max(part, axis=0, keepdims=True)
                    spot = pl.ds(start + k, 1), pl.ds(at, block)
                    max_ref[spot] = jnp.maximum(max_ref[spot], best) if fold else best
            return 0

        lax.fori_loop(0, count // step, group, 0, unroll=total <= block)

    best_of(other_ref, (1 - core) * half, False)
    fetch.wait()
    best_of(held_ref, core * half, True)
    put(jnp.sum(max_ref[...].T.reshape(total // q_tokens, q_tokens, count), axis=1), core, out_refs)


def score(core, doc_lens, pieces, doc_tokens, other, put, out_shapes):
    smem = pl.BlockSpec(memory_space=pltpu.SMEM)
    vmem = pl.BlockSpec(memory_space=pltpu.VMEM)
    hbm = pl.BlockSpec(memory_space=pltpu.HBM)
    count = doc_tokens.shape[0]
    queries = sum(p.shape[0] for p in pieces)
    q_tokens, width = pieces[0].shape[1:]
    doc_tokens = pltpu.with_memory_space_constraint(doc_tokens, pltpu.HBM)
    return pl.pallas_call(
        functools.partial(score_kernel, len(pieces), put),
        out_shape=[jax.ShapeDtypeStruct(shape, jnp.float32) for shape in out_shapes],
        in_specs=[smem, smem] + [vmem] * len(pieces) + [hbm, vmem],
        out_specs=[vmem] * len(out_shapes),
        scratch_shapes=[
            pltpu.VMEM((queries * q_tokens, width), jnp.bfloat16),
            pltpu.VMEM((count, queries * q_tokens), jnp.float32),
            pltpu.VMEM(doc_tokens.shape, jnp.bfloat16),
            pltpu.SemaphoreType.DMA(()),
        ],
        compiler_params=pltpu.CompilerParams(vmem_limit_bytes=(8 + queries // 16) * 1024 * 1024),
        name="score",
    )(core.reshape(1), doc_lens, *pieces, doc_tokens, other)


def pick_kernel(n_pieces, wide, base_ref, cand_ref, *refs):
    piece_refs, out_ref = refs[:n_pieces], refs[n_pieces]
    parts = [ref[...] for ref in piece_refs]
    parts = [part[:, t: t + wide] for group in zip(*[iter(parts)] * min(2, n_pieces))
             for t in range(0, parts[0].shape[1], wide) for part in group]
    table = jnp.concatenate(parts, axis=1) if len(parts) > 1 else parts[0]
    size = table.shape[1]
    rows, width = cand_ref.shape
    spot = jnp.bitwise_xor(cand_ref[...], base_ref[0])
    for at in range(0, width, LANES):
        wide = min(LANES, width - at)
        index = spot[:, at: at + wide]
        if wide < LANES:
            index = jnp.concatenate([index, jnp.zeros((rows, LANES - wide), jnp.int32)], axis=1)
        low = jnp.bitwise_and(index, LANES - 1)
        high = lax.shift_right_logical(index, LANES.bit_length() - 1)
        value = jnp.zeros((rows, LANES), jnp.float32)
        for t in range(0, size, LANES):
            found = jnp.take_along_axis(table[:, t: t + LANES], low, axis=1, mode="promise_in_bounds")
            value = jnp.where(high == t // LANES, found, value)
        out_ref[:, pl.ds(at, wide)] = value[:, :wide]


def pick(base, candidates, pieces, wide):
    smem = pl.BlockSpec(memory_space=pltpu.SMEM)
    vmem = pl.BlockSpec(memory_space=pltpu.VMEM)
    return pl.pallas_call(
        functools.partial(pick_kernel, len(pieces), wide),
        out_shape=jax.ShapeDtypeStruct(candidates.shape, jnp.float32),
        in_specs=[smem, vmem] + [vmem] * len(pieces),
        out_specs=vmem,
        compiler_params=pltpu.CompilerParams(vmem_limit_bytes=4 * 1024 * 1024),
        name="pick",
    )(base.reshape(1), candidates, *pieces)


SELF, NEAR, FAR = (0, 0), (1, 0), (2, 0)
NEAR_ACROSS, FAR_ACROSS = (1, 1), (2, 1)


def put_two_levels(scores, core, out_refs):
    kept_near_ref, kept_far_ref, lent_ref = out_refs
    q_each = kept_near_ref.shape[0]
    block = [scores[k * q_each: (k + 1) * q_each] for k in range(4)]
    zero = jnp.zeros_like(block[0])

    def left(x):
        return jnp.concatenate([x, zero], axis=1)

    def right(x):
        return jnp.concatenate([zero, x], axis=1)

    kept_near_ref[...] = jnp.where(core == 0, left(block[0]), right(block[0]))
    kept_far_ref[...] = left(block[1])
    lent_ref[pl.ds(0, q_each), :] = jnp.where(core == 0, right(block[2]), left(block[2]))
    lent_ref[pl.ds(q_each, q_each), :] = right(block[3])


def two_columns(queries, doc_tokens, doc_lens, candidates, core):
    q_owned = queries.shape[0]
    count = doc_tokens.shape[0]

    def exchange(array, step0, step1):
        pairs = []
        for z in range(4):
            for x in range(2):
                for d, (dz, dx) in enumerate((step0, step1)):
                    pairs.append(((z * 2 + x) * 2 + d, ((z ^ dz) * 2 + (x ^ dx)) * 2 + d))
        return lax.ppermute(array, ALL_AXES, pairs)

    def cross(array):
        return lax.ppermute(array, "dim", [(0, 1), (1, 0)])

    far = exchange(queries, FAR, FAR_ACROSS)
    near = exchange(queries, SELF, NEAR_ACROSS)
    first = jnp.concatenate([near, far], axis=0)
    first, docs_out = lax.optimization_barrier((first, doc_tokens))
    second = exchange(first, NEAR, NEAR)
    other = cross(docs_out)
    pair = (q_owned, 2 * count)
    kept_near, kept_far, lent = score(
        core, doc_lens, [first, second], doc_tokens, other, put_two_levels, [pair, pair, (2 * q_owned, 2 * count)]
    )
    brought = exchange(lent, NEAR, NEAR)
    far = exchange(kept_far + brought[q_owned:], FAR, FAR_ACROSS)
    near = exchange(kept_near + brought[:q_owned], SELF, NEAR_ACROSS)
    base = (lax.axis_index("shard") * 2 + (lax.axis_index("qgrp") ^ core)) * count
    return pick(base, candidates, [near, cross(near), far, cross(far)], count)


def any_columns(queries, doc_tokens, doc_lens, candidates, n, cores, core):
    q_owned = candidates.shape[0]
    count = doc_tokens.shape[0]
    gathered = lax.all_gather(queries, INDEX_AXES, axis=0, tiled=True)
    other = lax.ppermute(doc_tokens, "dim", [(s, cores - 1 - s) for s in range(cores)])

    def put(scores, core, out_refs):
        out_refs[0][...] = scores

    block = score(core, doc_lens, [gathered], doc_tokens, other, put, [(n * q_owned, count)])[0]
    moved = lax.all_to_all(
        block.reshape(n, q_owned, count), INDEX_AXES, split_axis=0, concat_axis=0, tiled=True
    )
    table = moved.transpose(1, 0, 2).reshape(q_owned, n * count)
    return pick(jnp.int32(0), candidates, [table], n * count)


def per_device(queries, doc_tokens, doc_lens, candidates):
    sizes = n_z, n_x, cores = tuple(lax.axis_size(axis) for axis in ALL_AXES)
    count = doc_tokens.shape[0]
    core = lax.axis_index("dim")
    if sizes == (4, 2, 2) and count & (count - 1) == 0:
        return two_columns(queries, doc_tokens, doc_lens, candidates, core)
    return any_columns(queries, doc_tokens, doc_lens, candidates, n_z * n_x, cores, core)


def solution(mesh):
    in_specs = (
        P(("groups",) + INDEX_AXES, None, None),
        P(("groups",) + INDEX_AXES, "dim", None),
        P(("groups",) + INDEX_AXES),
        P(("groups",) + INDEX_AXES, None),
    )
    out_specs = P(("groups",) + INDEX_AXES, None)
    return jax.shard_map(
        per_device, mesh=mesh, in_specs=in_specs, out_specs=out_specs, check_vma=False
    )
```

```python
import functools

import jax
import jax.numpy as jnp
from jax import lax
from jax.experimental import pallas as pl
from jax.experimental.pallas import tpu as pltpu
from jax.sharding import PartitionSpec as P

INDEX_AXES = ("shard", "qgrp")
ALL_AXES = ("shard", "qgrp", "dim")
LOW = -1e30
LANES = 128
BLOCK = 256


def score_kernel(n_pieces, put, me_ref, lens_ref, *refs):
    piece_refs = refs[:n_pieces]
    own_ref, other_ref = refs[n_pieces: n_pieces + 2]
    out_refs = refs[n_pieces + 2: -4]
    flat_ref, max_ref, held_ref, sem = refs[-4:]
    core = me_ref[0]
    q_tokens, width = piece_refs[0].shape[1:]
    count, half, _ = own_ref.shape
    total = flat_ref.shape[0]
    fetch = pltpu.make_async_copy(own_ref, held_ref, sem)
    fetch.start()
    at = 0
    for piece_ref in piece_refs:
        rows = piece_ref.shape[0] * q_tokens
        flat_ref[pl.ds(at, rows), :] = piece_ref[...].reshape(rows, width)
        at += rows
    block = min(total, BLOCK)
    step = min(count, 8)
    rows = lax.broadcasted_iota(jnp.int32, (half, block), 0)

    def best_of(ref, first, fold):
        def group(g, _):
            start = g * step
            docs = ref[pl.ds(start, step)].reshape(step * half, width)
            for at in range(0, total, block):
                flat = flat_ref[pl.ds(at, block), :]
                scores = lax.dot_general(
                    docs, flat, (((1,), (1,)), ((), ())), preferred_element_type=jnp.float32
                )
                for k in range(step):
                    part = scores[k * half: (k + 1) * half]
                    part = jnp.where(rows < lens_ref[start + k] - first, part, LOW)
                    best = jnp.max(part, axis=0, keepdims=True)
                    spot = pl.ds(start + k, 1), pl.ds(at, block)
                    max_ref[spot] = jnp.maximum(max_ref[spot], best) if fold else best
            return 0

        lax.fori_loop(0, count // step, group, 0, unroll=total <= block)

    best_of(other_ref, (1 - core) * half, False)
    fetch.wait()
    best_of(held_ref, core * half, True)
    put(jnp.sum(max_ref[...].T.reshape(total // q_tokens, q_tokens, count), axis=1), out_refs)


def score(core, doc_lens, pieces, doc_tokens, other, put, out_shapes):
    smem = pl.BlockSpec(memory_space=pltpu.SMEM)
    vmem = pl.BlockSpec(memory_space=pltpu.VMEM)
    hbm = pl.BlockSpec(memory_space=pltpu.HBM)
    count = doc_tokens.shape[0]
    queries = sum(p.shape[0] for p in pieces)
    q_tokens, width = pieces[0].shape[1:]
    doc_tokens = pltpu.with_memory_space_constraint(doc_tokens, pltpu.HBM)
    return pl.pallas_call(
        functools.partial(score_kernel, len(pieces), put),
        out_shape=[jax.ShapeDtypeStruct(shape, jnp.float32) for shape in out_shapes],
        in_specs=[smem, smem] + [vmem] * len(pieces) + [hbm, vmem],
        out_specs=[vmem] * len(out_shapes),
        scratch_shapes=[
            pltpu.VMEM((queries * q_tokens, width), jnp.bfloat16),
            pltpu.VMEM((count, queries * q_tokens), jnp.float32),
            pltpu.VMEM(doc_tokens.shape, jnp.bfloat16),
            pltpu.SemaphoreType.DMA(()),
        ],
        compiler_params=pltpu.CompilerParams(vmem_limit_bytes=(8 + queries // 16) * 1024 * 1024),
        name="score",
    )(core.reshape(1), doc_lens, *pieces, doc_tokens, other)


def pick_kernel(n_pieces, wide, base_ref, cand_ref, *refs):
    piece_refs, out_ref = refs[:n_pieces], refs[n_pieces]
    parts = [ref[...] for ref in piece_refs]
    parts = [part[:, t: t + wide] for group in zip(*[iter(parts)] * min(2, n_pieces))
             for t in range(0, parts[0].shape[1], wide) for part in group]
    table = jnp.concatenate(parts, axis=1) if len(parts) > 1 else parts[0]
    size = table.shape[1]
    rows, width = cand_ref.shape
    spot = jnp.bitwise_xor(cand_ref[...], base_ref[0])
    for at in range(0, width, LANES):
        wide = min(LANES, width - at)
        index = spot[:, at: at + wide]
        if wide < LANES:
            index = jnp.concatenate([index, jnp.zeros((rows, LANES - wide), jnp.int32)], axis=1)
        low = jnp.bitwise_and(index, LANES - 1)
        high = lax.shift_right_logical(index, LANES.bit_length() - 1)
        value = jnp.zeros((rows, LANES), jnp.float32)
        for t in range(0, size, LANES):
            found = jnp.take_along_axis(table[:, t: t + LANES], low, axis=1, mode="promise_in_bounds")
            value = jnp.where(high == t // LANES, found, value)
        out_ref[:, pl.ds(at, wide)] = value[:, :wide]


def pick(base, candidates, pieces, wide):
    smem = pl.BlockSpec(memory_space=pltpu.SMEM)
    vmem = pl.BlockSpec(memory_space=pltpu.VMEM)
    return pl.pallas_call(
        functools.partial(pick_kernel, len(pieces), wide),
        out_shape=jax.ShapeDtypeStruct(candidates.shape, jnp.float32),
        in_specs=[smem, vmem] + [vmem] * len(pieces),
        out_specs=vmem,
        compiler_params=pltpu.CompilerParams(vmem_limit_bytes=4 * 1024 * 1024),
        name="pick",
    )(base.reshape(1), candidates, *pieces)


NEAR, FAR = (1, 0), (2, 0)
NEAR_ACROSS, FAR_ACROSS = (1, 1), (2, 1)


def put_two_levels(scores, out_refs):
    kept_near_ref, kept_far_ref, lent_ref = out_refs
    q_each = kept_near_ref.shape[0]
    block = [scores[k * q_each: (k + 1) * q_each] for k in range(4)]
    zero = jnp.zeros_like(block[0])

    def left(x):
        return jnp.concatenate([x, zero], axis=1)

    def right(x):
        return jnp.concatenate([zero, x], axis=1)

    kept_near_ref[...] = right(block[0])
    kept_far_ref[...] = left(block[1])
    lent_ref[pl.ds(0, q_each), :] = left(block[2])
    lent_ref[pl.ds(q_each, q_each), :] = right(block[3])


def two_columns(queries, doc_tokens, doc_lens, candidates, core):
    q_owned = queries.shape[0]
    count = doc_tokens.shape[0]

    def exchange(array, step0, step1):
        pairs = []
        for z in range(4):
            for x in range(2):
                for d, (dz, dx) in enumerate((step0, step1)):
                    pairs.append(((z * 2 + x) * 2 + d, ((z ^ dz) * 2 + (x ^ dx)) * 2 + d))
        return lax.ppermute(array, ALL_AXES, pairs)

    def cross(array):
        return lax.ppermute(array, "dim", [(0, 1), (1, 0)])

    far = exchange(queries, FAR, FAR_ACROSS)
    near = exchange(queries, NEAR, NEAR_ACROSS)
    first = jnp.concatenate([near, far], axis=0)
    first, docs_out = lax.optimization_barrier((first, doc_tokens))
    second = exchange(first, NEAR, NEAR)
    other = cross(docs_out)
    pair = (q_owned, 2 * count)
    kept_near, kept_far, lent = score(
        core, doc_lens, [first, second], doc_tokens, other, put_two_levels, [pair, pair, (2 * q_owned, 2 * count)]
    )
    brought = exchange(lent, NEAR, NEAR)
    far = exchange(kept_far + brought[q_owned:], FAR, FAR_ACROSS)
    near = exchange(kept_near + brought[:q_owned], NEAR, NEAR_ACROSS)
    base = (lax.axis_index("shard") * 2 + (lax.axis_index("qgrp") ^ core)) * count
    return pick(base, candidates, [near, cross(near), far, cross(far)], count)


def any_columns(queries, doc_tokens, doc_lens, candidates, n, cores, core):
    q_owned = candidates.shape[0]
    count = doc_tokens.shape[0]
    gathered = lax.all_gather(queries, INDEX_AXES, axis=0, tiled=True)
    other = lax.ppermute(doc_tokens, "dim", [(s, cores - 1 - s) for s in range(cores)])

    def put(scores, out_refs):
        out_refs[0][...] = scores

    block = score(core, doc_lens, [gathered], doc_tokens, other, put, [(n * q_owned, count)])[0]
    moved = lax.all_to_all(
        block.reshape(n, q_owned, count), INDEX_AXES, split_axis=0, concat_axis=0, tiled=True
    )
    table = moved.transpose(1, 0, 2).reshape(q_owned, n * count)
    return pick(jnp.int32(0), candidates, [table], n * count)


def per_device(queries, doc_tokens, doc_lens, candidates):
    sizes = n_z, n_x, cores = tuple(lax.axis_size(axis) for axis in ALL_AXES)
    count = doc_tokens.shape[0]
    core = lax.axis_index("dim")
    if sizes == (4, 2, 2) and count & (count - 1) == 0:
        return two_columns(queries, doc_tokens, doc_lens, candidates, core)
    return any_columns(queries, doc_tokens, doc_lens, candidates, n_z * n_x, cores, core)


def solution(mesh):
    in_specs = (
        P(("groups",) + INDEX_AXES, None, None),
        P(("groups",) + INDEX_AXES, "dim", None),
        P(("groups",) + INDEX_AXES),
        P(("groups",) + INDEX_AXES, None),
    )
    out_specs = P(("groups",) + INDEX_AXES, None)
    return jax.shard_map(
        per_device, mesh=mesh, in_specs=in_specs, out_specs=out_specs, check_vma=False
    )
```

```python
import functools

import jax
import jax.numpy as jnp
from jax import lax
from jax.experimental import pallas as pl
from jax.experimental.pallas import tpu as pltpu
from jax.sharding import PartitionSpec as P

INDEX_AXES = ("shard", "qgrp")
ALL_AXES = ("shard", "qgrp", "dim")
LOW = -1e30
LANES = 128
BLOCK = 256


def score_kernel(n_pieces, with_own, put, me_ref, lens_ref, *refs):
    piece_refs = refs[:n_pieces]
    own_ref, other_ref = refs[n_pieces: n_pieces + 2]
    out_refs = refs[n_pieces + 2: -6]
    flat_ref, turned_ref, part_ref, max_ref, held_ref, sem = refs[-6:]
    core = me_ref[0]
    q_tokens, width = piece_refs[0].shape[1:]
    count, half, _ = own_ref.shape
    total = flat_ref.shape[0]
    fetch = pltpu.make_async_copy(own_ref, held_ref, sem)
    fetch.start()
    at = 0
    for k in range(n_pieces - int(with_own)):
        rows = piece_refs[k].shape[0] * q_tokens
        piece = piece_refs[k][...].reshape(rows, width)
        if with_own and k == n_pieces - 2:
            piece = jnp.where(core == 0, piece_refs[k + 1][...].reshape(rows, width), piece)
        flat_ref[pl.ds(at, rows), :] = piece
        at += rows
    turned_ref[...] = flat_ref[...].T
    block = min(total, BLOCK)
    step = min(count, 8)
    rows = lax.broadcasted_iota(jnp.int32, (half, LANES), 0)

    def best_of(ref, first, last):
        def group(g, _):
            start = g * step
            docs = ref[pl.ds(start, step)].reshape(step * half, width)
            for at in range(0, total, block):
                scores = jnp.dot(docs, turned_ref[:, pl.ds(at, block)], preferred_element_type=jnp.float32)
                for lane in range(0, block, LANES):
                    to = pl.ds(at + lane, LANES)
                    bests = []
                    for k in range(step):
                        part = scores[k * half: (k + 1) * half, lane: lane + LANES]
                        part = jnp.where(rows < lens_ref[start + k] - first, part, LOW)
                        best = jnp.max(part.reshape(half // 8, 8, LANES), axis=0)
                        spot = pl.ds(pl.multiple_of((start + k) * 8, 8), 8)
                        if last:
                            best = jnp.maximum(best, part_ref[spot, to])
                            bests.append(jnp.max(best, axis=0, keepdims=True))
                        else:
                            part_ref[spot, to] = best
                    if last:
                        max_ref[pl.ds(pl.multiple_of(start, step), step), to] = jnp.concatenate(bests, axis=0)
            return 0

        lax.fori_loop(0, count // step, group, 0, unroll=total <= block)

    best_of(other_ref, (1 - core) * half, False)
    fetch.wait()
    best_of(held_ref, core * half, True)
    put(jnp.sum(max_ref[...].T.reshape(total // q_tokens, q_tokens, count), axis=1), out_refs)


def score(core, doc_lens, pieces, doc_tokens, other, put, out_shapes, with_own):
    smem = pl.BlockSpec(memory_space=pltpu.SMEM)
    vmem = pl.BlockSpec(memory_space=pltpu.VMEM)
    hbm = pl.BlockSpec(memory_space=pltpu.HBM)
    count = doc_tokens.shape[0]
    queries = sum(p.shape[0] for p in pieces[int(with_own):])
    q_tokens, width = pieces[0].shape[1:]
    doc_tokens = pltpu.with_memory_space_constraint(doc_tokens, pltpu.HBM)
    return pl.pallas_call(
        functools.partial(score_kernel, len(pieces), with_own, put),
        out_shape=[jax.ShapeDtypeStruct(shape, jnp.float32) for shape in out_shapes],
        in_specs=[smem, smem] + [vmem] * len(pieces) + [hbm, vmem],
        out_specs=[vmem] * len(out_shapes),
        scratch_shapes=[
            pltpu.VMEM((queries * q_tokens, width), jnp.bfloat16),
            pltpu.VMEM((width, queries * q_tokens), jnp.bfloat16),
            pltpu.VMEM((count * 8, queries * q_tokens), jnp.float32),
            pltpu.VMEM((count, queries * q_tokens), jnp.float32),
            pltpu.VMEM(doc_tokens.shape, jnp.bfloat16),
            pltpu.SemaphoreType.DMA(()),
        ],
        compiler_params=pltpu.CompilerParams(vmem_limit_bytes=(8 + queries // 10) * 1024 * 1024),
        name="score",
    )(core.reshape(1), doc_lens, *pieces, doc_tokens, other)


def pick_kernel(n_pieces, wide, base_ref, cand_ref, *refs):
    piece_refs, out_ref = refs[:n_pieces], refs[n_pieces]
    parts = [ref[...] for ref in piece_refs]
    parts = [part[:, t: t + wide] for group in zip(*[iter(parts)] * min(2, n_pieces))
             for t in range(0, parts[0].shape[1], wide) for part in group]
    table = jnp.concatenate(parts, axis=1) if len(parts) > 1 else parts[0]
    size = table.shape[1]
    rows, width = cand_ref.shape
    spot = jnp.bitwise_xor(cand_ref[...], base_ref[0])
    for at in range(0, width, LANES):
        wide = min(LANES, width - at)
        index = spot[:, at: at + wide]
        if wide < LANES:
            index = jnp.concatenate([index, jnp.zeros((rows, LANES - wide), jnp.int32)], axis=1)
        low = jnp.bitwise_and(index, LANES - 1)
        high = lax.shift_right_logical(index, LANES.bit_length() - 1)
        value = jnp.zeros((rows, LANES), jnp.float32)
        for t in range(0, size, LANES):
            found = jnp.take_along_axis(table[:, t: t + LANES], low, axis=1, mode="promise_in_bounds")
            value = jnp.where(high == t // LANES, found, value)
        out_ref[:, pl.ds(at, wide)] = value[:, :wide]


def pick(base, candidates, pieces, wide):
    smem = pl.BlockSpec(memory_space=pltpu.SMEM)
    vmem = pl.BlockSpec(memory_space=pltpu.VMEM)
    return pl.pallas_call(
        functools.partial(pick_kernel, len(pieces), wide),
        out_shape=jax.ShapeDtypeStruct(candidates.shape, jnp.float32),
        in_specs=[smem, vmem] + [vmem] * len(pieces),
        out_specs=vmem,
        compiler_params=pltpu.CompilerParams(vmem_limit_bytes=4 * 1024 * 1024),
        name="pick",
    )(base.reshape(1), candidates, *pieces)


def two_columns(queries, doc_tokens, doc_lens, candidates, n_z, core):
    q_owned = queries.shape[0]
    count = doc_tokens.shape[0]

    def exchange(array, dz, dx0, dx1):
        pairs = [
            ((z * 2 + x) * 2 + d, ((z ^ dz) * 2 + (x ^ dx)) * 2 + d)
            for z in range(n_z) for x in range(2) for d, dx in enumerate((dx0, dx1))
        ]
        return lax.ppermute(array, ALL_AXES, pairs)

    def cross(array):
        return lax.ppermute(array, "dim", [(0, 1), (1, 0)])

    other = cross(doc_tokens)
    far_first = list(reversed(range(n_z)))
    pieces = [exchange(queries, dz, int(dz == 0), 1) for dz in far_first]

    def put(scores, out_refs):
        for k, out_ref in enumerate(out_refs):
            out_ref[...] = scores[k * q_owned: (k + 1) * q_owned]

    blocks = score(core, doc_lens, pieces + [queries], doc_tokens, other, put, [(q_owned, count)] * n_z, True)
    table = []
    for dz, block in zip(far_first, blocks):
        moved = exchange(block, dz, int(dz == 0), 1)
        if dz == 0:
            moved = jnp.where(core == 0, block, moved)
        table += [moved, cross(moved)]
    base = ((lax.axis_index("shard") ^ (n_z - 1)) * 2 + (lax.axis_index("qgrp") ^ core)) * count
    return pick(base, candidates, table, count)


def any_columns(queries, doc_tokens, doc_lens, candidates, n, cores, core):
    q_owned = candidates.shape[0]
    count = doc_tokens.shape[0]
    gathered = lax.all_gather(queries, INDEX_AXES, axis=0, tiled=True)
    other = lax.ppermute(doc_tokens, "dim", [(s, cores - 1 - s) for s in range(cores)])

    def put(scores, out_refs):
        out_refs[0][...] = scores

    block = score(core, doc_lens, [gathered], doc_tokens, other, put, [(n * q_owned, count)], False)[0]
    moved = lax.all_to_all(
        block.reshape(n, q_owned, count), INDEX_AXES, split_axis=0, concat_axis=0, tiled=True
    )
    table = moved.transpose(1, 0, 2).reshape(q_owned, n * count)
    return pick(jnp.int32(0), candidates, [table], n * count)


def per_device(queries, doc_tokens, doc_lens, candidates):
    sizes = n_z, n_x, cores = tuple(lax.axis_size(axis) for axis in ALL_AXES)
    count = doc_tokens.shape[0]
    core = lax.axis_index("dim")
    if sizes in ((4, 2, 2), (2, 2, 2)) and count & (count - 1) == 0:
        return two_columns(queries, doc_tokens, doc_lens, candidates, n_z, core)
    return any_columns(queries, doc_tokens, doc_lens, candidates, n_z * n_x, cores, core)


def solution(mesh):
    in_specs = (
        P(("groups",) + INDEX_AXES, None, None),
        P(("groups",) + INDEX_AXES, "dim", None),
        P(("groups",) + INDEX_AXES),
        P(("groups",) + INDEX_AXES, None),
    )
    out_specs = P(("groups",) + INDEX_AXES, None)
    return jax.shard_map(
        per_device, mesh=mesh, in_specs=in_specs, out_specs=out_specs, check_vma=False
    )
```

```python
import functools

import jax
import jax.numpy as jnp
from jax import lax
from jax.experimental import pallas as pl
from jax.experimental.pallas import tpu as pltpu
from jax.sharding import PartitionSpec as P

INDEX_AXES = ("shard", "qgrp")
ALL_AXES = ("shard", "qgrp", "dim")
LOW = -1e30
LANES = 128
BLOCK = 256


def score_kernel(n_pieces, with_own, put, me_ref, lens_ref, *refs):
    piece_refs = refs[:n_pieces]
    own_ref, other_ref = refs[n_pieces: n_pieces + 2]
    out_refs = refs[n_pieces + 2: -6]
    flat_ref, turned_ref, part_ref, max_ref, held_ref, sem = refs[-6:]
    core = me_ref[0]
    q_tokens, width = piece_refs[0].shape[1:]
    count, half, _ = own_ref.shape
    total = flat_ref.shape[0]
    fetch = pltpu.make_async_copy(own_ref, held_ref, sem)
    fetch.start()
    at = 0
    for k in range(n_pieces - int(with_own)):
        rows = piece_refs[k].shape[0] * q_tokens
        piece = piece_refs[k][...].reshape(rows, width)
        if with_own and k == n_pieces - 2:
            piece = jnp.where(core == 0, piece_refs[k + 1][...].reshape(rows, width), piece)
        flat_ref[pl.ds(at, rows), :] = piece
        at += rows
    turned_ref[...] = flat_ref[...].T
    block = min(total, BLOCK)
    step = min(count, 8)
    rows = lax.broadcasted_iota(jnp.int32, (half, LANES), 0)

    def best_of(ref, first, last):
        def group(g, _):
            start = g * step
            docs = ref[pl.ds(start, step)].reshape(step * half, width)
            for at in range(0, total, block):
                scores = jnp.dot(docs, turned_ref[:, pl.ds(at, block)], preferred_element_type=jnp.float32)
                for lane in range(0, block, LANES):
                    to = pl.ds(at + lane, LANES)
                    bests = []
                    for k in range(step):
                        part = scores[k * half: (k + 1) * half, lane: lane + LANES]
                        part = jnp.where(rows < lens_ref[start + k] - first, part, LOW)
                        best = jnp.max(part.reshape(half // 8, 8, LANES), axis=0)
                        spot = pl.ds(pl.multiple_of((start + k) * 8, 8), 8)
                        if last:
                            best = jnp.maximum(best, part_ref[spot, to])
                            bests.append(jnp.max(best, axis=0, keepdims=True))
                        else:
                            part_ref[spot, to] = best
                    if last:
                        max_ref[pl.ds(pl.multiple_of(start, step), step), to] = jnp.concatenate(bests, axis=0)
            return 0

        lax.fori_loop(0, count // step, group, 0, unroll=total <= block)

    best_of(other_ref, (1 - core) * half, False)
    fetch.wait()
    best_of(held_ref, core * half, True)
    put(jnp.sum(max_ref[...].T.reshape(total // q_tokens, q_tokens, count), axis=1), out_refs)


def score(core, doc_lens, pieces, doc_tokens, other, put, out_shapes, with_own):
    smem = pl.BlockSpec(memory_space=pltpu.SMEM)
    vmem = pl.BlockSpec(memory_space=pltpu.VMEM)
    hbm = pl.BlockSpec(memory_space=pltpu.HBM)
    count = doc_tokens.shape[0]
    queries = sum(p.shape[0] for p in pieces[int(with_own):])
    q_tokens, width = pieces[0].shape[1:]
    doc_tokens = pltpu.with_memory_space_constraint(doc_tokens, pltpu.HBM)
    return pl.pallas_call(
        functools.partial(score_kernel, len(pieces), with_own, put),
        out_shape=[jax.ShapeDtypeStruct(shape, jnp.float32) for shape in out_shapes],
        in_specs=[smem, smem] + [vmem] * len(pieces) + [hbm, vmem],
        out_specs=[vmem] * len(out_shapes),
        scratch_shapes=[
            pltpu.VMEM((queries * q_tokens, width), jnp.bfloat16),
            pltpu.VMEM((width, queries * q_tokens), jnp.bfloat16),
            pltpu.VMEM((count * 8, queries * q_tokens), jnp.float32),
            pltpu.VMEM((count, queries * q_tokens), jnp.float32),
            pltpu.VMEM(doc_tokens.shape, jnp.bfloat16),
            pltpu.SemaphoreType.DMA(()),
        ],
        compiler_params=pltpu.CompilerParams(vmem_limit_bytes=(8 + queries // 10) * 1024 * 1024),
        name="score",
    )(core.reshape(1), doc_lens, *pieces, doc_tokens, other)


def pick_kernel(n_pieces, wide, base_ref, cand_ref, *refs):
    piece_refs, out_ref = refs[:n_pieces], refs[n_pieces]
    parts = [ref[...] for ref in piece_refs]
    parts = [part[:, t: t + wide] for group in zip(*[iter(parts)] * min(2, n_pieces))
             for t in range(0, parts[0].shape[1], wide) for part in group]
    table = jnp.concatenate(parts, axis=1) if len(parts) > 1 else parts[0]
    size = table.shape[1]
    rows, width = cand_ref.shape
    spot = jnp.bitwise_xor(cand_ref[...], base_ref[0])
    for at in range(0, width, LANES):
        wide = min(LANES, width - at)
        index = spot[:, at: at + wide]
        if wide < LANES:
            index = jnp.concatenate([index, jnp.zeros((rows, LANES - wide), jnp.int32)], axis=1)
        low = jnp.bitwise_and(index, LANES - 1)
        high = lax.shift_right_logical(index, LANES.bit_length() - 1)
        value = jnp.zeros((rows, LANES), jnp.float32)
        for t in range(0, size, LANES):
            found = jnp.take_along_axis(table[:, t: t + LANES], low, axis=1, mode="promise_in_bounds")
            value = jnp.where(high == t // LANES, found, value)
        out_ref[:, pl.ds(at, wide)] = value[:, :wide]


def pick(base, candidates, pieces, wide):
    smem = pl.BlockSpec(memory_space=pltpu.SMEM)
    vmem = pl.BlockSpec(memory_space=pltpu.VMEM)
    return pl.pallas_call(
        functools.partial(pick_kernel, len(pieces), wide),
        out_shape=jax.ShapeDtypeStruct(candidates.shape, jnp.float32),
        in_specs=[smem, vmem] + [vmem] * len(pieces),
        out_specs=vmem,
        compiler_params=pltpu.CompilerParams(vmem_limit_bytes=4 * 1024 * 1024),
        name="pick",
    )(base.reshape(1), candidates, *pieces)


def two_columns(queries, doc_tokens, doc_lens, candidates, n_z, core):
    q_owned = queries.shape[0]
    count = doc_tokens.shape[0]

    def exchange(array, dz, dx0, dx1):
        pairs = [
            ((z * 2 + x) * 2 + d, ((z ^ dz) * 2 + (x ^ dx)) * 2 + d)
            for z in range(n_z) for x in range(2) for d, dx in enumerate((dx0, dx1))
        ]
        return lax.ppermute(array, ALL_AXES, pairs)

    def cross(array):
        return lax.ppermute(array, "dim", [(0, 1), (1, 0)])

    other = cross(doc_tokens)
    far_first = list(reversed(range(n_z)))
    pieces = [exchange(queries, dz, int(dz == 0), 1) for dz in far_first]

    def put(scores, out_refs):
        for k, out_ref in enumerate(out_refs):
            out_ref[...] = scores[k * q_owned: (k + 1) * q_owned]

    blocks = score(core, doc_lens, pieces + [queries], doc_tokens, other, put, [(q_owned, count)] * n_z, True)
    table = []
    for dz, block in zip(reversed(far_first), reversed(blocks)):
        moved = jnp.where(core == -dz, block, exchange(block, dz, int(dz == 0), 1))
        table += [moved, cross(moved)]
    base = (lax.axis_index("shard") * 2 + (lax.axis_index("qgrp") ^ core)) * count
    return pick(base, candidates, table, count)


def any_columns(queries, doc_tokens, doc_lens, candidates, n, cores, core):
    q_owned = candidates.shape[0]
    count = doc_tokens.shape[0]
    gathered = lax.all_gather(queries, INDEX_AXES, axis=0, tiled=True)
    other = lax.ppermute(doc_tokens, "dim", [(s, cores - 1 - s) for s in range(cores)])

    def put(scores, out_refs):
        out_refs[0][...] = scores

    block = score(core, doc_lens, [gathered], doc_tokens, other, put, [(n * q_owned, count)], False)[0]
    moved = lax.all_to_all(
        block.reshape(n, q_owned, count), INDEX_AXES, split_axis=0, concat_axis=0, tiled=True
    )
    table = moved.transpose(1, 0, 2).reshape(q_owned, n * count)
    return pick(jnp.int32(0), candidates, [table], n * count)


def per_device(queries, doc_tokens, doc_lens, candidates):
    sizes = n_z, n_x, cores = tuple(lax.axis_size(axis) for axis in ALL_AXES)
    count = doc_tokens.shape[0]
    core = lax.axis_index("dim")
    if sizes in ((4, 2, 2), (2, 2, 2)) and count & (count - 1) == 0:
        return two_columns(queries, doc_tokens, doc_lens, candidates, n_z, core)
    return any_columns(queries, doc_tokens, doc_lens, candidates, n_z * n_x, cores, core)


def solution(mesh):
    in_specs = (
        P(("groups",) + INDEX_AXES, None, None),
        P(("groups",) + INDEX_AXES, "dim", None),
        P(("groups",) + INDEX_AXES),
        P(("groups",) + INDEX_AXES, None),
    )
    out_specs = P(("groups",) + INDEX_AXES, None)
    return jax.shard_map(
        per_device, mesh=mesh, in_specs=in_specs, out_specs=out_specs, check_vma=False
    )
```

```python
import functools

import jax
import jax.numpy as jnp
from jax import lax
from jax.experimental import pallas as pl
from jax.experimental.pallas import tpu as pltpu
from jax.sharding import PartitionSpec as P

INDEX_AXES = ("shard", "qgrp")
ALL_AXES = ("shard", "qgrp", "dim")
LANES = 128
BLOCK = 256


def stage_kernel(core_ref, lens_ref, own_ref, other_ref, own_out, other_out, held_ref, sem):
    core = core_ref[0]
    count, half, width = own_ref.shape
    fetch = pltpu.make_async_copy(own_ref, held_ref, sem)
    fetch.start()
    fetch.wait()
    rows = lax.broadcasted_iota(jnp.int32, (half, width), 0)
    step = min(count, 4)

    def group(g, _):
        for k in range(step):
            p = g * step + k
            own = held_ref[p].astype(jnp.float32)
            other = other_ref[p].astype(jnp.float32)
            first = jnp.where(core == 0, own[:1], other[:1])
            length = lens_ref[p]
            own_out[p] = jnp.where(rows < length - core * half, own, first).astype(own_out.dtype)
            other_out[p] = jnp.where(rows < length - (1 - core) * half, other, first).astype(own_out.dtype)
        return 0

    lax.fori_loop(0, count // step, group, 0)


def stage(core, doc_lens, doc_tokens, other):
    smem = pl.BlockSpec(memory_space=pltpu.SMEM)
    vmem = pl.BlockSpec(memory_space=pltpu.VMEM)
    hbm = pl.BlockSpec(memory_space=pltpu.HBM)
    doc_tokens = pltpu.with_memory_space_constraint(doc_tokens, pltpu.HBM)
    return pl.pallas_call(
        stage_kernel,
        out_shape=[jax.ShapeDtypeStruct(doc_tokens.shape, doc_tokens.dtype)] * 2,
        in_specs=[smem, smem, hbm, vmem],
        out_specs=[vmem] * 2,
        scratch_shapes=[pltpu.VMEM(doc_tokens.shape, doc_tokens.dtype), pltpu.SemaphoreType.DMA(())],
        compiler_params=pltpu.CompilerParams(vmem_limit_bytes=8 * 1024 * 1024),
        cost_estimate=pl.CostEstimate(flops=4 * doc_tokens.size, bytes_accessed=8 * doc_tokens.size, transcendentals=0),
        name="stage",
    )(core.reshape(1), doc_lens, doc_tokens, other)


def score_kernel(n_pieces, put, *refs):
    piece_refs = refs[:n_pieces]
    own_ref, other_ref = refs[n_pieces: n_pieces + 2]
    out_refs = refs[n_pieces + 2: -3]
    flat_ref, turned_ref, max_ref = refs[-3:]
    q_tokens, width = piece_refs[0].shape[1:]
    count, half, _ = own_ref.shape
    total = flat_ref.shape[0]
    at = 0
    for piece_ref in piece_refs:
        rows = piece_ref.shape[0] * q_tokens
        flat_ref[pl.ds(at, rows), :] = piece_ref[...].reshape(rows, width)
        at += rows
    turned_ref[...] = flat_ref[...].T
    block = min(total, BLOCK)
    step = min(count, 8)

    def group(g, _):
        start = pl.multiple_of(g * step, step)
        for at in range(0, total, block):
            best = None
            for ref in (own_ref, other_ref):
                docs = ref[pl.ds(start, step)].reshape(step * half, width)
                part = jnp.dot(docs, turned_ref[:, pl.ds(at, block)], preferred_element_type=jnp.float32)
                part = jnp.max(part.reshape(step, half // 8, 8, block), axis=1)
                best = part if best is None else jnp.maximum(best, part)
            max_ref[pl.ds(start, step), pl.ds(at, block)] = jnp.max(best, axis=1)
        return 0

    lax.fori_loop(0, count // step, group, 0, unroll=total <= block)
    put(jnp.sum(max_ref[...].T.reshape(total // q_tokens, q_tokens, count), axis=1), out_refs)


def score(pieces, own, other, put, out_shapes):
    vmem = pl.BlockSpec(memory_space=pltpu.VMEM)
    count = own.shape[0]
    queries = sum(p.shape[0] for p in pieces)
    q_tokens, width = pieces[0].shape[1:]
    return pl.pallas_call(
        functools.partial(score_kernel, len(pieces), put),
        out_shape=[jax.ShapeDtypeStruct(shape, jnp.float32) for shape in out_shapes],
        in_specs=[vmem] * (len(pieces) + 2),
        out_specs=[vmem] * len(out_shapes),
        scratch_shapes=[
            pltpu.VMEM((queries * q_tokens, width), jnp.bfloat16),
            pltpu.VMEM((width, queries * q_tokens), jnp.bfloat16),
            pltpu.VMEM((count, queries * q_tokens), jnp.float32),
        ],
        compiler_params=pltpu.CompilerParams(vmem_limit_bytes=(8 + queries // 10) * 1024 * 1024),
        name="score",
    )(*pieces, own, other)


def pick_kernel(n_pieces, wide, spot_ref, *refs):
    piece_refs, out_ref = refs[:n_pieces], refs[n_pieces]
    parts = [ref[...] for ref in piece_refs]
    parts = [part[:, t: t + wide] for group in zip(*[iter(parts)] * min(2, n_pieces))
             for t in range(0, parts[0].shape[1], wide) for part in group]
    table = jnp.concatenate(parts, axis=1) if len(parts) > 1 else parts[0]
    size = table.shape[1]
    rows, width = spot_ref.shape
    spot = spot_ref[...]
    for at in range(0, width, LANES):
        wide = min(LANES, width - at)
        index = spot[:, at: at + wide]
        if wide < LANES:
            index = jnp.concatenate([index, jnp.zeros((rows, LANES - wide), jnp.int32)], axis=1)
        low = jnp.bitwise_and(index, LANES - 1)
        high = lax.shift_right_logical(index, LANES.bit_length() - 1)
        value = jnp.zeros((rows, LANES), jnp.float32)
        for t in range(0, size, LANES):
            found = jnp.take_along_axis(table[:, t: t + LANES], low, axis=1, mode="promise_in_bounds")
            value = jnp.where(high == t // LANES, found, value)
        out_ref[:, pl.ds(at, wide)] = value[:, :wide]


def pick(spots, pieces, wide):
    vmem = pl.BlockSpec(memory_space=pltpu.VMEM)
    return pl.pallas_call(
        functools.partial(pick_kernel, len(pieces), wide),
        out_shape=jax.ShapeDtypeStruct(spots.shape, jnp.float32),
        in_specs=[vmem] * (1 + len(pieces)),
        out_specs=vmem,
        compiler_params=pltpu.CompilerParams(vmem_limit_bytes=4 * 1024 * 1024),
        name="pick",
    )(spots, *pieces)


def two_columns(queries, doc_tokens, doc_lens, candidates, n_z, core):
    q_owned = queries.shape[0]
    count = doc_tokens.shape[0]

    def exchange(array, dz, dx0, dx1):
        pairs = [
            ((z * 2 + x) * 2 + d, ((z ^ dz) * 2 + (x ^ dx)) * 2 + d)
            for z in range(n_z) for x in range(2) for d, dx in enumerate((dx0, dx1))
        ]
        return lax.ppermute(array, ALL_AXES, pairs)

    def cross(array):
        return lax.ppermute(array, "dim", [(0, 1), (1, 0)])

    other = cross(doc_tokens)
    def from_column(array):
        pairs = []
        for z in range(n_z):
            for x in range(2):
                pairs.append(((z * 2 + x) * 2, (z * 2 + 1 - x) * 2 + 1))
                pairs.append(((z * 2 + x) * 2 + 1, (z * 2 + x) * 2))
        return lax.ppermute(array, ALL_AXES, pairs)

    far_first = list(reversed(range(n_z)))
    pieces = [exchange(queries, dz, 0, 1) for dz in far_first[:-1]] + [from_column(queries)]
    own, other = stage(core, doc_lens, doc_tokens, other)

    def put(scores, out_refs):
        for k, out_ref in enumerate(out_refs):
            out_ref[...] = scores[k * q_owned: (k + 1) * q_owned]

    blocks = score(pieces, own, other, put, [(q_owned, count)] * n_z)
    table = []
    for dz, block in zip(reversed(far_first), reversed(blocks)):
        moved = jnp.where(core == -dz, block, exchange(block, dz, int(dz == 0), 1))
        table += [moved, cross(moved)]
    base = (lax.axis_index("shard") * 2 + (lax.axis_index("qgrp") ^ core)) * count
    return pick(candidates ^ base, table, count)


def any_columns(queries, doc_tokens, doc_lens, candidates, n, cores, core):
    q_owned = candidates.shape[0]
    count = doc_tokens.shape[0]
    gathered = lax.all_gather(queries, INDEX_AXES, axis=0, tiled=True)
    other = lax.ppermute(doc_tokens, "dim", [(s, cores - 1 - s) for s in range(cores)])

    def put(scores, out_refs):
        out_refs[0][...] = scores

    own, other = stage(core, doc_lens, doc_tokens, other)
    block = score([gathered], own, other, put, [(n * q_owned, count)])[0]
    moved = lax.all_to_all(
        block.reshape(n, q_owned, count), INDEX_AXES, split_axis=0, concat_axis=0, tiled=True
    )
    table = moved.transpose(1, 0, 2).reshape(q_owned, n * count)
    return pick(candidates, [table], n * count)


def per_device(queries, doc_tokens, doc_lens, candidates):
    sizes = n_z, n_x, cores = tuple(lax.axis_size(axis) for axis in ALL_AXES)
    count = doc_tokens.shape[0]
    core = lax.axis_index("dim")
    if sizes in ((4, 2, 2), (2, 2, 2)) and count & (count - 1) == 0:
        return two_columns(queries, doc_tokens, doc_lens, candidates, n_z, core)
    return any_columns(queries, doc_tokens, doc_lens, candidates, n_z * n_x, cores, core)


def solution(mesh):
    in_specs = (
        P(("groups",) + INDEX_AXES, None, None),
        P(("groups",) + INDEX_AXES, "dim", None),
        P(("groups",) + INDEX_AXES),
        P(("groups",) + INDEX_AXES, None),
    )
    out_specs = P(("groups",) + INDEX_AXES, None)
    return jax.shard_map(
        per_device, mesh=mesh, in_specs=in_specs, out_specs=out_specs, check_vma=False
    )
```

```python
import functools

import jax
import jax.numpy as jnp
from jax import lax
from jax.experimental import pallas as pl
from jax.experimental.pallas import tpu as pltpu
from jax.sharding import PartitionSpec as P

INDEX_AXES = ("shard", "qgrp")
ALL_AXES = ("shard", "qgrp", "dim")
LANES = 128
BLOCK = 256


def stage_kernel(lens_hbm_ref, own_ref, other_ref, own_out, other_out, lens_ref, held_ref, lens_sem, sems):
    core = lax.axis_index("dim")
    count, half, width = own_ref.shape
    chunks = sems.shape[0]
    size = count // chunks
    lens_copy = pltpu.make_async_copy(lens_hbm_ref, lens_ref, lens_sem)
    lens_copy.start()
    fetches = []
    for c in range(chunks):
        part = pl.ds(c * size, size)
        fetches.append(pltpu.make_async_copy(own_ref.at[part], held_ref.at[part], sems.at[c]))
        fetches[-1].start()
    rows = lax.broadcasted_iota(jnp.int32, (half, width), 0).astype(jnp.int16)
    lens_copy.wait()
    for c in range(chunks):
        fetches[c].wait()

        def one(k, _):
            p = c * size + k
            own, other = held_ref[p], other_ref[p]
            first = jnp.where(core == 0, own[:1], other[:1])
            length = lens_ref[p]
            own_valid = rows < (length - core * half).astype(jnp.int16)
            other_valid = rows < (length - (1 - core) * half).astype(jnp.int16)
            own_out[p] = jnp.where(own_valid, own, first)
            other_out[p] = jnp.where(other_valid, other, first)
            return 0

        lax.fori_loop(0, size, one, 0, unroll=True)


def stage(doc_lens, doc_tokens, other):
    vmem = pl.BlockSpec(memory_space=pltpu.VMEM)
    hbm = pl.BlockSpec(memory_space=pltpu.HBM)
    doc_tokens = pltpu.with_memory_space_constraint(doc_tokens, pltpu.HBM)
    doc_lens = pltpu.with_memory_space_constraint(doc_lens, pltpu.HBM)
    count = doc_tokens.shape[0]
    chunks = 4 if count % 4 == 0 else 1
    return pl.pallas_call(
        stage_kernel,
        out_shape=[jax.ShapeDtypeStruct(doc_tokens.shape, doc_tokens.dtype)] * 2,
        in_specs=[hbm, hbm, vmem],
        out_specs=[vmem] * 2,
        scratch_shapes=[
            pltpu.SMEM(doc_lens.shape, jnp.int32),
            pltpu.VMEM(doc_tokens.shape, doc_tokens.dtype),
            pltpu.SemaphoreType.DMA(()),
            pltpu.SemaphoreType.DMA((chunks,)),
        ],
        compiler_params=pltpu.CompilerParams(vmem_limit_bytes=8 * 1024 * 1024),
        cost_estimate=pl.CostEstimate(flops=4 * doc_tokens.size, bytes_accessed=8 * doc_tokens.size, transcendentals=0),
        name="stage",
    )(doc_lens, doc_tokens, other)


def score_kernel(n_pieces, put, *refs):
    piece_refs = refs[:n_pieces]
    own_ref, other_ref = refs[n_pieces: n_pieces + 2]
    out_refs = refs[n_pieces + 2: -3]
    flat_ref, turned_ref, max_ref = refs[-3:]
    q_tokens, width = piece_refs[0].shape[1:]
    count, half, _ = own_ref.shape
    total = flat_ref.shape[0]
    at = 0
    for piece_ref in piece_refs:
        rows = piece_ref.shape[0] * q_tokens
        flat_ref[pl.ds(at, rows), :] = piece_ref[...].reshape(rows, width)
        at += rows
    turned_ref[...] = flat_ref[...].T
    block = min(total, BLOCK)
    step = min(count, 8)

    def group(g, _):
        start = pl.multiple_of(g * step, step)
        for at in range(0, total, block):
            best = None
            for ref in (own_ref, other_ref):
                docs = ref[pl.ds(start, step)].reshape(step * half, width)
                part = jnp.dot(docs, turned_ref[:, pl.ds(at, block)], preferred_element_type=jnp.float32)
                part = jnp.max(part.reshape(step, half // 8, 8, block), axis=1)
                best = part if best is None else jnp.maximum(best, part)
            max_ref[pl.ds(start, step), pl.ds(at, block)] = jnp.max(best, axis=1)
        return 0

    lax.fori_loop(0, count // step, group, 0, unroll=total <= block)
    put(jnp.sum(max_ref[...].T.reshape(total // q_tokens, q_tokens, count), axis=1), out_refs)


def score(pieces, own, other, put, out_shapes):
    vmem = pl.BlockSpec(memory_space=pltpu.VMEM)
    count = own.shape[0]
    queries = sum(p.shape[0] for p in pieces)
    q_tokens, width = pieces[0].shape[1:]
    return pl.pallas_call(
        functools.partial(score_kernel, len(pieces), put),
        out_shape=[jax.ShapeDtypeStruct(shape, jnp.float32) for shape in out_shapes],
        in_specs=[vmem] * (len(pieces) + 2),
        out_specs=[vmem] * len(out_shapes),
        scratch_shapes=[
            pltpu.VMEM((queries * q_tokens, width), jnp.bfloat16),
            pltpu.VMEM((width, queries * q_tokens), jnp.bfloat16),
            pltpu.VMEM((count, queries * q_tokens), jnp.float32),
        ],
        compiler_params=pltpu.CompilerParams(vmem_limit_bytes=(8 + queries // 10) * 1024 * 1024),
        name="score",
    )(*pieces, own, other)


def pick_kernel(order, spot_ref, *refs):
    out_ref = refs[len(order)]
    parts = [refs[k][...] for k in order]
    table = jnp.concatenate(parts, axis=1) if len(parts) > 1 else parts[0]
    size = table.shape[1]
    rows, width = spot_ref.shape
    spot = spot_ref[...]
    for at in range(0, width, LANES):
        wide = min(LANES, width - at)
        index = spot[:, at: at + wide]
        if wide < LANES:
            index = jnp.concatenate([index, jnp.zeros((rows, LANES - wide), jnp.int32)], axis=1)
        low = jnp.bitwise_and(index, LANES - 1)
        high = lax.shift_right_logical(index, LANES.bit_length() - 1)
        value = jnp.zeros((rows, LANES), jnp.float32)
        for t in range(0, size, LANES):
            found = jnp.take_along_axis(table[:, t: t + LANES], low, axis=1, mode="promise_in_bounds")
            value = jnp.where(high == t // LANES, found, value)
        out_ref[:, pl.ds(at, wide)] = value[:, :wide]


def pick(spots, pieces, order):
    vmem = pl.BlockSpec(memory_space=pltpu.VMEM)
    return pl.pallas_call(
        functools.partial(pick_kernel, order),
        out_shape=jax.ShapeDtypeStruct(spots.shape, jnp.float32),
        in_specs=[vmem] * (1 + len(pieces)),
        out_specs=vmem,
        compiler_params=pltpu.CompilerParams(vmem_limit_bytes=4 * 1024 * 1024),
        name="pick",
    )(spots, *pieces)


def two_columns(queries, doc_tokens, doc_lens, candidates, core):
    q_owned = queries.shape[0]
    count = doc_tokens.shape[0]

    def exchange(array, dz, dx0, dx1):
        pairs = [
            ((z * 2 + x) * 2 + d, ((z ^ dz) * 2 + (x ^ dx)) * 2 + d)
            for z in range(4) for x in range(2) for d, dx in enumerate((dx0, dx1))
        ]
        return lax.ppermute(array, ALL_AXES, pairs)

    def cross(array):
        return lax.ppermute(array, "dim", [(0, 1), (1, 0)])

    other = cross(doc_tokens)
    def from_column(array):
        pairs = []
        for z in range(4):
            for x in range(2):
                pairs.append(((z * 2 + x) * 2, (z * 2 + 1 - x) * 2 + 1))
                pairs.append(((z * 2 + x) * 2 + 1, (z * 2 + x) * 2))
        return lax.ppermute(array, ALL_AXES, pairs)

    steps = (2, 3, 1, 0)
    pieces = [exchange(queries, dz, 0, 1) if dz else from_column(queries) for dz in steps]
    own, other = stage(doc_lens, doc_tokens, other)

    def put(scores, out_refs):
        for k, out_ref in enumerate(out_refs):
            out_ref[...] = scores[k * q_owned: (k + 1) * q_owned]

    blocks = score(pieces, own, other, put, [(q_owned, count)] * 4)
    blocks = dict(zip(steps, blocks))
    steps = (1, 0, 2, 3)
    table = []
    for dz in steps:
        moved = jnp.where(core == -dz, blocks[dz], exchange(blocks[dz], dz, int(dz == 0), 1))
        table += [moved, cross(moved)]
    order = [2 * steps.index(dz) + side for dz in range(4) for side in range(2)]
    base = (lax.axis_index("shard") * 2 + (lax.axis_index("qgrp") ^ core)) * count
    return pick(candidates ^ base, table, order)


def any_columns(queries, doc_tokens, doc_lens, candidates, n, cores, core):
    q_owned = candidates.shape[0]
    count = doc_tokens.shape[0]
    gathered = lax.all_gather(queries, INDEX_AXES, axis=0, tiled=True)
    other = lax.ppermute(doc_tokens, "dim", [(s, cores - 1 - s) for s in range(cores)])

    def put(scores, out_refs):
        out_refs[0][...] = scores

    own, other = stage(doc_lens, doc_tokens, other)
    block = score([gathered], own, other, put, [(n * q_owned, count)])[0]
    moved = lax.all_to_all(
        block.reshape(n, q_owned, count), INDEX_AXES, split_axis=0, concat_axis=0, tiled=True
    )
    table = moved.transpose(1, 0, 2).reshape(q_owned, n * count)
    return pick(candidates, [table], [0])


def per_device(queries, doc_tokens, doc_lens, candidates):
    sizes = n_z, n_x, cores = tuple(lax.axis_size(axis) for axis in ALL_AXES)
    count = doc_tokens.shape[0]
    core = lax.axis_index("dim")
    if sizes == (4, 2, 2) and count & (count - 1) == 0:
        return two_columns(queries, doc_tokens, doc_lens, candidates, core)
    return any_columns(queries, doc_tokens, doc_lens, candidates, n_z * n_x, cores, core)


def solution(mesh):
    in_specs = (
        P(("groups",) + INDEX_AXES, None, None),
        P(("groups",) + INDEX_AXES, "dim", None),
        P(("groups",) + INDEX_AXES),
        P(("groups",) + INDEX_AXES, None),
    )
    out_specs = P(("groups",) + INDEX_AXES, None)
    return jax.shard_map(
        per_device, mesh=mesh, in_specs=in_specs, out_specs=out_specs, check_vma=False
    )
```

```python
import functools

import jax
import jax.numpy as jnp
from jax import lax
from jax.experimental import pallas as pl
from jax.experimental.pallas import tpu as pltpu
from jax.sharding import PartitionSpec as P

INDEX_AXES = ("shard", "qgrp")
ALL_AXES = ("shard", "qgrp", "dim")
LANES = 128
BLOCK = 256
ISSUE = (0, 1, 2, 3)
OPERANDS = (4, 5, 6, 7, 0, 1, 2, 3)


def stage_kernel(lens_hbm_ref, own_ref, other_ref, own_out, other_out, lens_ref, held_ref, lens_sem, sems):
    core = lax.axis_index("dim")
    count, half, width = own_ref.shape
    chunks = sems.shape[0]
    size = count // chunks
    lens_copy = pltpu.make_async_copy(lens_hbm_ref, lens_ref, lens_sem)
    lens_copy.start()
    fetches = []
    for c in range(chunks):
        part = pl.ds(c * size, size)
        fetches.append(pltpu.make_async_copy(own_ref.at[part], held_ref.at[part], sems.at[c]))
        fetches[-1].start()
    rows = lax.broadcasted_iota(jnp.int32, (half, width), 0).astype(jnp.int16)
    lens_copy.wait()
    for c in range(chunks):
        fetches[c].wait()

        def one(k, _):
            p = c * size + k
            own, other = held_ref[p], other_ref[p]
            first = jnp.where(core == 0, own[:1], other[:1])
            length = lens_ref[p]
            own_valid = rows < (length - core * half).astype(jnp.int16)
            other_valid = rows < (length - (1 - core) * half).astype(jnp.int16)
            own_out[p] = jnp.where(own_valid, own, first)
            other_out[p] = jnp.where(other_valid, other, first)
            return 0

        lax.fori_loop(0, size, one, 0, unroll=True)


def stage(doc_lens, doc_tokens, other):
    vmem = pl.BlockSpec(memory_space=pltpu.VMEM)
    hbm = pl.BlockSpec(memory_space=pltpu.HBM)
    doc_tokens = pltpu.with_memory_space_constraint(doc_tokens, pltpu.HBM)
    doc_lens = pltpu.with_memory_space_constraint(doc_lens, pltpu.HBM)
    count = doc_tokens.shape[0]
    chunks = 4 if count % 4 == 0 else 1
    return pl.pallas_call(
        stage_kernel,
        out_shape=[jax.ShapeDtypeStruct(doc_tokens.shape, doc_tokens.dtype)] * 2,
        in_specs=[hbm, hbm, vmem],
        out_specs=[vmem] * 2,
        scratch_shapes=[
            pltpu.SMEM(doc_lens.shape, jnp.int32),
            pltpu.VMEM(doc_tokens.shape, doc_tokens.dtype),
            pltpu.SemaphoreType.DMA(()),
            pltpu.SemaphoreType.DMA((chunks,)),
        ],
        compiler_params=pltpu.CompilerParams(vmem_limit_bytes=8 * 1024 * 1024),
        cost_estimate=pl.CostEstimate(flops=4 * doc_tokens.size, bytes_accessed=8 * doc_tokens.size, transcendentals=0),
        name="stage",
    )(doc_lens, doc_tokens, other)


def score_kernel(n_pieces, put, *refs):
    piece_refs = refs[:n_pieces]
    own_ref, other_ref = refs[n_pieces: n_pieces + 2]
    out_refs = refs[n_pieces + 2: -3]
    flat_ref, turned_ref, max_ref = refs[-3:]
    q_tokens, width = piece_refs[0].shape[1:]
    count, half, _ = own_ref.shape
    total = flat_ref.shape[0]
    at = 0
    for piece_ref in piece_refs:
        rows = piece_ref.shape[0] * q_tokens
        flat_ref[pl.ds(at, rows), :] = piece_ref[...].reshape(rows, width)
        at += rows
    turned_ref[...] = flat_ref[...].T
    block = min(total, BLOCK)
    step = min(count, 8)

    def group(g, _):
        start = pl.multiple_of(g * step, step)
        for at in range(0, total, block):
            best = None
            for ref in (own_ref, other_ref):
                docs = ref[pl.ds(start, step)].reshape(step * half, width)
                part = jnp.dot(docs, turned_ref[:, pl.ds(at, block)], preferred_element_type=jnp.float32)
                part = jnp.max(part.reshape(step, half // 8, 8, block), axis=1)
                best = part if best is None else jnp.maximum(best, part)
            max_ref[pl.ds(start, step), pl.ds(at, block)] = jnp.max(best, axis=1)
        return 0

    lax.fori_loop(0, count // step, group, 0, unroll=total <= block)
    put(jnp.sum(max_ref[...].T.reshape(total // q_tokens, q_tokens, count), axis=1), out_refs)


def score(pieces, own, other, put, out_shapes):
    vmem = pl.BlockSpec(memory_space=pltpu.VMEM)
    count = own.shape[0]
    queries = sum(p.shape[0] for p in pieces)
    q_tokens, width = pieces[0].shape[1:]
    return pl.pallas_call(
        functools.partial(score_kernel, len(pieces), put),
        out_shape=[jax.ShapeDtypeStruct(shape, jnp.float32) for shape in out_shapes],
        in_specs=[vmem] * (len(pieces) + 2),
        out_specs=[vmem] * len(out_shapes),
        scratch_shapes=[
            pltpu.VMEM((queries * q_tokens, width), jnp.bfloat16),
            pltpu.VMEM((width, queries * q_tokens), jnp.bfloat16),
            pltpu.VMEM((count, queries * q_tokens), jnp.float32),
        ],
        compiler_params=pltpu.CompilerParams(vmem_limit_bytes=(8 + queries // 10) * 1024 * 1024),
        name="score",
    )(*pieces, own, other)


def pick_kernel(order, spot_ref, *refs):
    out_ref = refs[len(order)]
    parts = [refs[k][...] for k in order]
    table = jnp.concatenate(parts, axis=1) if len(parts) > 1 else parts[0]
    size = table.shape[1]
    rows, width = spot_ref.shape
    spot = spot_ref[...]
    for at in range(0, width, LANES):
        wide = min(LANES, width - at)
        index = spot[:, at: at + wide]
        if wide < LANES:
            index = jnp.concatenate([index, jnp.zeros((rows, LANES - wide), jnp.int32)], axis=1)
        low = jnp.bitwise_and(index, LANES - 1)
        high = lax.shift_right_logical(index, LANES.bit_length() - 1)
        value = jnp.zeros((rows, LANES), jnp.float32)
        for t in range(0, size, LANES):
            found = jnp.take_along_axis(table[:, t: t + LANES], low, axis=1, mode="promise_in_bounds")
            value = jnp.where(high == t // LANES, found, value)
        out_ref[:, pl.ds(at, wide)] = value[:, :wide]


def pick(spots, pieces, order):
    vmem = pl.BlockSpec(memory_space=pltpu.VMEM)
    return pl.pallas_call(
        functools.partial(pick_kernel, order),
        out_shape=jax.ShapeDtypeStruct(spots.shape, jnp.float32),
        in_specs=[vmem] * (1 + len(pieces)),
        out_specs=vmem,
        compiler_params=pltpu.CompilerParams(vmem_limit_bytes=4 * 1024 * 1024),
        name="pick",
    )(spots, *pieces)


QUERY_STEPS = (((0, 1), (3, 0), 1), ((2, 1), (3, 1), 1), ((2, 0), (1, 1), 1), (None, (1, 0), 1))
SCORE_STEPS = (((2, 1), (3, 1), 0), ((2, 0), (3, 0), 1), ((0, 1), (1, 1), 0), (None, (1, 0), 1))


def move(array, steps, owner_sends):
    pairs = []
    for z in range(4):
        for x in range(2):
            for core in range(2):
                dz, dx = steps[core] or (0, 0)
                here = (z * 2 + x) * 2 + core
                owner = ((z ^ dz) * 2 + (x ^ dx)) * 2 + (core ^ steps[2])
                pairs.append((owner, here) if owner_sends else (here, owner))
    return lax.ppermute(array, ALL_AXES, pairs)


def four_by_two(queries, doc_tokens, doc_lens, candidates, core):
    q_owned = queries.shape[0]
    count = doc_tokens.shape[0]

    def cross(array):
        return lax.ppermute(array, "dim", [(0, 1), (1, 0)])

    other = cross(doc_tokens)
    pieces = [move(queries, steps, True) for steps in QUERY_STEPS]
    own, other = stage(doc_lens, doc_tokens, other)
    origin = [[[q[c] for q in QUERY_STEPS].index(steps[c]) for c in range(2)] for steps in SCORE_STEPS]

    def put(scores, out_refs):
        core = lax.axis_index("dim")
        block = [scores[k * q_owned: (k + 1) * q_owned] for k in range(4)]
        for (k0, k1), out_ref in zip(origin, out_refs):
            out_ref[...] = block[k0] if k0 == k1 else jnp.where(core == 0, block[k0], block[k1])

    blocks = score(pieces, own, other, put, [(q_owned, count)] * 4)
    table = [None] * 8
    for k in ISSUE:
        moved = move(blocks[k], SCORE_STEPS[k], False)
        table[2 * k: 2 * k + 2] = [moved, cross(moved)]
    groups = 0
    for k, steps in enumerate(SCORE_STEPS):
        for c in range(2):
            dz, dx = steps[c] or (0, 0)
            groups |= (2 * k + (c ^ steps[2])) << (3 * (2 * dz + dx))
    chip = lax.axis_index("shard") * 2 + lax.axis_index("qgrp")
    step = lax.shift_right_logical(candidates, count.bit_length() - 1) ^ chip
    group = (lax.shift_right_logical(jnp.full_like(step, groups), 3 * step) & 7) ^ core
    spots = group * count + (candidates & (count - 1))
    return pick(spots, [table[k] for k in OPERANDS], [OPERANDS.index(k) for k in range(8)])


def any_columns(queries, doc_tokens, doc_lens, candidates, n, cores, core):
    q_owned = candidates.shape[0]
    count = doc_tokens.shape[0]
    gathered = lax.all_gather(queries, INDEX_AXES, axis=0, tiled=True)
    other = lax.ppermute(doc_tokens, "dim", [(s, cores - 1 - s) for s in range(cores)])

    def put(scores, out_refs):
        out_refs[0][...] = scores

    own, other = stage(doc_lens, doc_tokens, other)
    block = score([gathered], own, other, put, [(n * q_owned, count)])[0]
    moved = lax.all_to_all(
        block.reshape(n, q_owned, count), INDEX_AXES, split_axis=0, concat_axis=0, tiled=True
    )
    table = moved.transpose(1, 0, 2).reshape(q_owned, n * count)
    return pick(candidates, [table], [0])


def per_device(queries, doc_tokens, doc_lens, candidates):
    sizes = n_z, n_x, cores = tuple(lax.axis_size(axis) for axis in ALL_AXES)
    count = doc_tokens.shape[0]
    core = lax.axis_index("dim")
    if sizes == (4, 2, 2) and count & (count - 1) == 0:
        return four_by_two(queries, doc_tokens, doc_lens, candidates, core)
    return any_columns(queries, doc_tokens, doc_lens, candidates, n_z * n_x, cores, core)


def solution(mesh):
    in_specs = (
        P(("groups",) + INDEX_AXES, None, None),
        P(("groups",) + INDEX_AXES, "dim", None),
        P(("groups",) + INDEX_AXES),
        P(("groups",) + INDEX_AXES, None),
    )
    out_specs = P(("groups",) + INDEX_AXES, None)
    return jax.shard_map(
        per_device, mesh=mesh, in_specs=in_specs, out_specs=out_specs, check_vma=False
    )
```

```python
import functools

import jax
import jax.numpy as jnp
from jax import lax
from jax.experimental import pallas as pl
from jax.experimental.pallas import tpu as pltpu
from jax.sharding import PartitionSpec as P

INDEX_AXES = ("shard", "qgrp")
ALL_AXES = ("shard", "qgrp", "dim")
LANES = 128
BLOCK = 256
ISSUE = (0, 1, 2, 3)
OPERANDS = (4, 5, 6, 7, 0, 1, 2, 3)


def stage_kernel(lens_hbm_ref, own_ref, other_ref, own_out, other_out, lens_ref, held_ref, lens_sem, sems):
    core = lax.axis_index("dim")
    count, half, width = own_ref.shape
    chunks = sems.shape[0]
    size = count // chunks
    lens_copy = pltpu.make_async_copy(lens_hbm_ref, lens_ref, lens_sem)
    lens_copy.start()
    fetches = []
    for c in range(chunks):
        part = pl.ds(c * size, size)
        fetches.append(pltpu.make_async_copy(own_ref.at[part], held_ref.at[part], sems.at[c]))
        fetches[-1].start()
    rows = lax.broadcasted_iota(jnp.int32, (half, width), 0).astype(jnp.int16)
    lens_copy.wait()
    for c in range(chunks):
        fetches[c].wait()

        def one(k, _):
            p = c * size + k
            own, other = held_ref[p], other_ref[p]
            first = jnp.where(core == 0, own[:1], other[:1])
            length = lens_ref[p]
            own_valid = rows < (length - core * half).astype(jnp.int16)
            other_valid = rows < (length - (1 - core) * half).astype(jnp.int16)
            own_out[p] = jnp.where(own_valid, own, first)
            other_out[p] = jnp.where(other_valid, other, first)
            return 0

        lax.fori_loop(0, size, one, 0, unroll=True)


def stage(doc_lens, doc_tokens, other):
    vmem = pl.BlockSpec(memory_space=pltpu.VMEM)
    hbm = pl.BlockSpec(memory_space=pltpu.HBM)
    doc_tokens = pltpu.with_memory_space_constraint(doc_tokens, pltpu.HBM)
    doc_lens = pltpu.with_memory_space_constraint(doc_lens, pltpu.HBM)
    count = doc_tokens.shape[0]
    chunks = 4 if count % 4 == 0 else 1
    return pl.pallas_call(
        stage_kernel,
        out_shape=[jax.ShapeDtypeStruct(doc_tokens.shape, doc_tokens.dtype)] * 2,
        in_specs=[hbm, hbm, vmem],
        out_specs=[vmem] * 2,
        scratch_shapes=[
            pltpu.SMEM(doc_lens.shape, jnp.int32),
            pltpu.VMEM(doc_tokens.shape, doc_tokens.dtype),
            pltpu.SemaphoreType.DMA(()),
            pltpu.SemaphoreType.DMA((chunks,)),
        ],
        compiler_params=pltpu.CompilerParams(vmem_limit_bytes=8 * 1024 * 1024),
        cost_estimate=pl.CostEstimate(flops=4 * doc_tokens.size, bytes_accessed=8 * doc_tokens.size, transcendentals=0),
        name="stage",
    )(doc_lens, doc_tokens, other)


def score_kernel(n_pieces, put, *refs):
    piece_refs = refs[:n_pieces]
    own_ref, other_ref = refs[n_pieces: n_pieces + 2]
    out_refs = refs[n_pieces + 2: -2]
    flat_ref, max_ref = refs[-2:]
    q_tokens, width = piece_refs[0].shape[1:]
    count, half, _ = own_ref.shape
    total = flat_ref.shape[0]
    at = 0
    for piece_ref in piece_refs:
        rows = piece_ref.shape[0] * q_tokens
        flat_ref[pl.ds(at, rows), :] = piece_ref[...].reshape(rows, width)
        at += rows
    block = min(total, BLOCK)
    step = min(count, 8)

    def group(g, _):
        start = pl.multiple_of(g * step, step)
        for at in range(0, total, block):
            best = None
            for ref in (own_ref, other_ref):
                docs = ref[pl.ds(start, step)].reshape(step * half, width)
                part = lax.dot_general(
                    docs, flat_ref[pl.ds(at, block), :], (((1,), (1,)), ((), ())), preferred_element_type=jnp.float32
                )
                part = jnp.max(part.reshape(step, half // 8, 8, block), axis=1)
                best = part if best is None else jnp.maximum(best, part)
            max_ref[pl.ds(start, step), pl.ds(at, block)] = jnp.max(best, axis=1)
        return 0

    lax.fori_loop(0, count // step, group, 0, unroll=total <= block)
    put(jnp.sum(max_ref[...].T.reshape(total // q_tokens, q_tokens, count), axis=1), out_refs)


def score(pieces, own, other, put, out_shapes):
    vmem = pl.BlockSpec(memory_space=pltpu.VMEM)
    count = own.shape[0]
    queries = sum(p.shape[0] for p in pieces)
    q_tokens, width = pieces[0].shape[1:]
    return pl.pallas_call(
        functools.partial(score_kernel, len(pieces), put),
        out_shape=[jax.ShapeDtypeStruct(shape, jnp.float32) for shape in out_shapes],
        in_specs=[vmem] * (len(pieces) + 2),
        out_specs=[vmem] * len(out_shapes),
        scratch_shapes=[
            pltpu.VMEM((queries * q_tokens, width), jnp.bfloat16),
            pltpu.VMEM((count, queries * q_tokens), jnp.float32),
        ],
        compiler_params=pltpu.CompilerParams(vmem_limit_bytes=(8 + queries // 10) * 1024 * 1024),
        name="score",
    )(*pieces, own, other)


def pick_kernel(order, spot_ref, *refs):
    out_ref = refs[len(order)]
    parts = [refs[k][...] for k in order]
    table = jnp.concatenate(parts, axis=1) if len(parts) > 1 else parts[0]
    size = table.shape[1]
    rows, width = spot_ref.shape
    spot = spot_ref[...]
    for at in range(0, width, LANES):
        wide = min(LANES, width - at)
        index = spot[:, at: at + wide]
        if wide < LANES:
            index = jnp.concatenate([index, jnp.zeros((rows, LANES - wide), jnp.int32)], axis=1)
        low = jnp.bitwise_and(index, LANES - 1)
        high = lax.shift_right_logical(index, LANES.bit_length() - 1)
        value = jnp.zeros((rows, LANES), jnp.float32)
        for t in range(0, size, LANES):
            found = jnp.take_along_axis(table[:, t: t + LANES], low, axis=1, mode="promise_in_bounds")
            value = jnp.where(high == t // LANES, found, value)
        out_ref[:, pl.ds(at, wide)] = value[:, :wide]


def pick(spots, pieces, order):
    vmem = pl.BlockSpec(memory_space=pltpu.VMEM)
    return pl.pallas_call(
        functools.partial(pick_kernel, order),
        out_shape=jax.ShapeDtypeStruct(spots.shape, jnp.float32),
        in_specs=[vmem] * (1 + len(pieces)),
        out_specs=vmem,
        compiler_params=pltpu.CompilerParams(vmem_limit_bytes=4 * 1024 * 1024),
        name="pick",
    )(spots, *pieces)


QUERY_STEPS = (((0, 1), (3, 0), 1), ((2, 1), (3, 1), 1), ((2, 0), (1, 1), 1), (None, (1, 0), 1))
SCORE_STEPS = (((2, 1), (3, 1), 0), ((2, 0), (3, 0), 1), ((0, 1), (1, 1), 0), (None, (1, 0), 1))


def move(array, steps, owner_sends):
    pairs = []
    for z in range(4):
        for x in range(2):
            for core in range(2):
                dz, dx = steps[core] or (0, 0)
                here = (z * 2 + x) * 2 + core
                owner = ((z ^ dz) * 2 + (x ^ dx)) * 2 + (core ^ steps[2])
                pairs.append((owner, here) if owner_sends else (here, owner))
    return lax.ppermute(array, ALL_AXES, pairs)


def four_by_two(queries, doc_tokens, doc_lens, candidates, core):
    q_owned = queries.shape[0]
    count = doc_tokens.shape[0]

    def cross(array):
        return lax.ppermute(array, "dim", [(0, 1), (1, 0)])

    other = cross(doc_tokens)
    pieces = [move(queries, steps, True) for steps in QUERY_STEPS]
    own, other = stage(doc_lens, doc_tokens, other)
    origin = [[[q[c] for q in QUERY_STEPS].index(steps[c]) for c in range(2)] for steps in SCORE_STEPS]

    def put(scores, out_refs):
        core = lax.axis_index("dim")
        block = [scores[k * q_owned: (k + 1) * q_owned] for k in range(4)]
        for (k0, k1), out_ref in zip(origin, out_refs):
            out_ref[...] = block[k0] if k0 == k1 else jnp.where(core == 0, block[k0], block[k1])

    blocks = score(pieces, own, other, put, [(q_owned, count)] * 4)
    table = [None] * 8
    for k in ISSUE:
        moved = move(blocks[k], SCORE_STEPS[k], False)
        table[2 * k: 2 * k + 2] = [moved, cross(moved)]
    groups = 0
    for k, steps in enumerate(SCORE_STEPS):
        for c in range(2):
            dz, dx = steps[c] or (0, 0)
            groups |= (2 * k + (c ^ steps[2])) << (3 * (2 * dz + dx))
    chip = lax.axis_index("shard") * 2 + lax.axis_index("qgrp")
    step = lax.shift_right_logical(candidates, count.bit_length() - 1) ^ chip
    group = (lax.shift_right_logical(jnp.full_like(step, groups), 3 * step) & 7) ^ core
    spots = group * count + (candidates & (count - 1))
    return pick(spots, [table[k] for k in OPERANDS], [OPERANDS.index(k) for k in range(8)])


def any_columns(queries, doc_tokens, doc_lens, candidates, n, cores, core):
    q_owned = candidates.shape[0]
    count = doc_tokens.shape[0]
    gathered = lax.all_gather(queries, INDEX_AXES, axis=0, tiled=True)
    other = lax.ppermute(doc_tokens, "dim", [(s, cores - 1 - s) for s in range(cores)])

    def put(scores, out_refs):
        out_refs[0][...] = scores

    own, other = stage(doc_lens, doc_tokens, other)
    block = score([gathered], own, other, put, [(n * q_owned, count)])[0]
    moved = lax.all_to_all(
        block.reshape(n, q_owned, count), INDEX_AXES, split_axis=0, concat_axis=0, tiled=True
    )
    table = moved.transpose(1, 0, 2).reshape(q_owned, n * count)
    return pick(candidates, [table], [0])


def per_device(queries, doc_tokens, doc_lens, candidates):
    sizes = n_z, n_x, cores = tuple(lax.axis_size(axis) for axis in ALL_AXES)
    count = doc_tokens.shape[0]
    core = lax.axis_index("dim")
    if sizes == (4, 2, 2) and count & (count - 1) == 0:
        return four_by_two(queries, doc_tokens, doc_lens, candidates, core)
    return any_columns(queries, doc_tokens, doc_lens, candidates, n_z * n_x, cores, core)


def solution(mesh):
    in_specs = (
        P(("groups",) + INDEX_AXES, None, None),
        P(("groups",) + INDEX_AXES, "dim", None),
        P(("groups",) + INDEX_AXES),
        P(("groups",) + INDEX_AXES, None),
    )
    out_specs = P(("groups",) + INDEX_AXES, None)
    return jax.shard_map(
        per_device, mesh=mesh, in_specs=in_specs, out_specs=out_specs, check_vma=False
    )
```

```python
import functools

import jax
import jax.numpy as jnp
from jax import lax
from jax.experimental import pallas as pl
from jax.experimental.pallas import tpu as pltpu
from jax.sharding import PartitionSpec as P

INDEX_AXES = ("shard", "qgrp")
ALL_AXES = ("shard", "qgrp", "dim")
LANES = 128
BLOCK = 256
ISSUE = (0, 1, 2, 3)
OPERANDS = (4, 5, 6, 7, 0, 1, 2, 3)


def stage_kernel(lens_hbm_ref, own_ref, other_ref, own_out, other_out, lens_ref, held_ref, lens_sem, sems):
    core = lax.axis_index("dim")
    count, half, width = own_ref.shape
    chunks = sems.shape[0]
    size = count // chunks
    lens_copy = pltpu.make_async_copy(lens_hbm_ref, lens_ref, lens_sem)
    lens_copy.start()
    fetches = []
    for c in range(chunks):
        part = pl.ds(c * size, size)
        fetches.append(pltpu.make_async_copy(own_ref.at[part], held_ref.at[part], sems.at[c]))
        fetches[-1].start()
    rows = lax.broadcasted_iota(jnp.int32, (half, width), 0).astype(jnp.int16)
    lens_copy.wait()
    for c in range(chunks):
        fetches[c].wait()

        def one(k, _):
            p = c * size + k
            own, other = held_ref[p], other_ref[p]
            first = jnp.where(core == 0, own[:1], other[:1])
            length = lens_ref[p]
            own_valid = rows < (length - core * half).astype(jnp.int16)
            other_valid = rows < (length - (1 - core) * half).astype(jnp.int16)
            own_out[p] = jnp.where(own_valid, own, first)
            other_out[p] = jnp.where(other_valid, other, first)
            return 0

        lax.fori_loop(0, size, one, 0, unroll=True)


def stage(doc_lens, doc_tokens, other):
    vmem = pl.BlockSpec(memory_space=pltpu.VMEM)
    hbm = pl.BlockSpec(memory_space=pltpu.HBM)
    doc_tokens = pltpu.with_memory_space_constraint(doc_tokens, pltpu.HBM)
    doc_lens = pltpu.with_memory_space_constraint(doc_lens, pltpu.HBM)
    count = doc_tokens.shape[0]
    chunks = 4 if count % 4 == 0 else 1
    return pl.pallas_call(
        stage_kernel,
        out_shape=[jax.ShapeDtypeStruct(doc_tokens.shape, doc_tokens.dtype)] * 2,
        in_specs=[hbm, hbm, vmem],
        out_specs=[vmem] * 2,
        scratch_shapes=[
            pltpu.SMEM(doc_lens.shape, jnp.int32),
            pltpu.VMEM(doc_tokens.shape, doc_tokens.dtype),
            pltpu.SemaphoreType.DMA(()),
            pltpu.SemaphoreType.DMA((chunks,)),
        ],
        compiler_params=pltpu.CompilerParams(vmem_limit_bytes=8 * 1024 * 1024),
        cost_estimate=pl.CostEstimate(flops=4 * doc_tokens.size, bytes_accessed=8 * doc_tokens.size, transcendentals=0),
        name="stage",
    )(doc_lens, doc_tokens, other)


def score_kernel(n_pieces, put, *refs):
    piece_refs = refs[:n_pieces]
    own_ref, other_ref = refs[n_pieces: n_pieces + 2]
    out_refs = refs[n_pieces + 2: -2]
    flat_ref, max_ref = refs[-2:]
    q_tokens, width = piece_refs[0].shape[1:]
    count, half, _ = own_ref.shape
    total = flat_ref.shape[0]
    at = 0
    for piece_ref in piece_refs:
        rows = piece_ref.shape[0] * q_tokens
        flat_ref[pl.ds(at, rows), :] = piece_ref[...].reshape(rows, width)
        at += rows
    block = min(total, BLOCK)
    step = min(count, 16)

    def group(g, _):
        start = pl.multiple_of(g * step, step)
        for at in range(0, total, block):
            best = None
            for ref in (own_ref, other_ref):
                docs = ref[pl.ds(start, step)].reshape(step * half, width)
                part = lax.dot_general(
                    docs, flat_ref[pl.ds(at, block), :], (((1,), (1,)), ((), ())), preferred_element_type=jnp.float32
                )
                part = jnp.max(part.reshape(step, half // 8, 8, block), axis=1)
                best = part if best is None else jnp.maximum(best, part)
            max_ref[pl.ds(start, step), pl.ds(at, block)] = jnp.max(best, axis=1)
        return 0

    lax.fori_loop(0, count // step, group, 0, unroll=total <= block)
    put(jnp.sum(max_ref[...].T.reshape(total // q_tokens, q_tokens, count), axis=1), out_refs)


def score(pieces, own, other, put, out_shapes):
    vmem = pl.BlockSpec(memory_space=pltpu.VMEM)
    count = own.shape[0]
    queries = sum(p.shape[0] for p in pieces)
    q_tokens, width = pieces[0].shape[1:]
    return pl.pallas_call(
        functools.partial(score_kernel, len(pieces), put),
        out_shape=[jax.ShapeDtypeStruct(shape, jnp.float32) for shape in out_shapes],
        in_specs=[vmem] * (len(pieces) + 2),
        out_specs=[vmem] * len(out_shapes),
        scratch_shapes=[
            pltpu.VMEM((queries * q_tokens, width), jnp.bfloat16),
            pltpu.VMEM((count, queries * q_tokens), jnp.float32),
        ],
        compiler_params=pltpu.CompilerParams(vmem_limit_bytes=(8 + queries // 10) * 1024 * 1024),
        name="score",
    )(*pieces, own, other)


def pick_kernel(order, spot_ref, *refs):
    out_ref = refs[len(order)]
    parts = [refs[k][...] for k in order]
    table = jnp.concatenate(parts, axis=1) if len(parts) > 1 else parts[0]
    size = table.shape[1]
    rows, width = spot_ref.shape
    spot = spot_ref[...]
    for at in range(0, width, LANES):
        wide = min(LANES, width - at)
        index = spot[:, at: at + wide]
        if wide < LANES:
            index = jnp.concatenate([index, jnp.zeros((rows, LANES - wide), jnp.int32)], axis=1)
        low = jnp.bitwise_and(index, LANES - 1)
        high = lax.shift_right_logical(index, LANES.bit_length() - 1)
        value = jnp.zeros((rows, LANES), jnp.float32)
        for t in range(0, size, LANES):
            found = jnp.take_along_axis(table[:, t: t + LANES], low, axis=1, mode="promise_in_bounds")
            value = jnp.where(high == t // LANES, found, value)
        out_ref[:, pl.ds(at, wide)] = value[:, :wide]


def pick(spots, pieces, order):
    vmem = pl.BlockSpec(memory_space=pltpu.VMEM)
    return pl.pallas_call(
        functools.partial(pick_kernel, order),
        out_shape=jax.ShapeDtypeStruct(spots.shape, jnp.float32),
        in_specs=[vmem] * (1 + len(pieces)),
        out_specs=vmem,
        compiler_params=pltpu.CompilerParams(vmem_limit_bytes=4 * 1024 * 1024),
        name="pick",
    )(spots, *pieces)


QUERY_STEPS = (((0, 1), (3, 0), 1), ((2, 1), (3, 1), 1), ((2, 0), (1, 1), 1), (None, (1, 0), 1))
SCORE_STEPS = (((2, 1), (3, 1), 0), ((2, 0), (3, 0), 1), ((0, 1), (1, 1), 0), (None, (1, 0), 1))


def move(array, steps, owner_sends):
    pairs = []
    for z in range(4):
        for x in range(2):
            for core in range(2):
                dz, dx = steps[core] or (0, 0)
                here = (z * 2 + x) * 2 + core
                owner = ((z ^ dz) * 2 + (x ^ dx)) * 2 + (core ^ steps[2])
                pairs.append((owner, here) if owner_sends else (here, owner))
    return lax.ppermute(array, ALL_AXES, pairs)


def four_by_two(queries, doc_tokens, doc_lens, candidates, core):
    q_owned = queries.shape[0]
    count = doc_tokens.shape[0]

    def cross(array):
        return lax.ppermute(array, "dim", [(0, 1), (1, 0)])

    other = cross(doc_tokens)
    pieces = [move(queries, steps, True) for steps in QUERY_STEPS]
    own, other = stage(doc_lens, doc_tokens, other)
    origin = [[[q[c] for q in QUERY_STEPS].index(steps[c]) for c in range(2)] for steps in SCORE_STEPS]

    def put(scores, out_refs):
        core = lax.axis_index("dim")
        block = [scores[k * q_owned: (k + 1) * q_owned] for k in range(4)]
        for (k0, k1), out_ref in zip(origin, out_refs):
            out_ref[...] = block[k0] if k0 == k1 else jnp.where(core == 0, block[k0], block[k1])

    blocks = score(pieces, own, other, put, [(q_owned, count)] * 4)
    table = [None] * 8
    for k in ISSUE:
        moved = move(blocks[k], SCORE_STEPS[k], False)
        table[2 * k: 2 * k + 2] = [moved, cross(moved)]
    groups = 0
    for k, steps in enumerate(SCORE_STEPS):
        for c in range(2):
            dz, dx = steps[c] or (0, 0)
            groups |= (2 * k + (c ^ steps[2])) << (3 * (2 * dz + dx))
    chip = lax.axis_index("shard") * 2 + lax.axis_index("qgrp")
    step = lax.shift_right_logical(candidates, count.bit_length() - 1) ^ chip
    group = (lax.shift_right_logical(jnp.full_like(step, groups), 3 * step) & 7) ^ core
    spots = group * count + (candidates & (count - 1))
    return pick(spots, [table[k] for k in OPERANDS], [OPERANDS.index(k) for k in range(8)])


def any_columns(queries, doc_tokens, doc_lens, candidates, n, cores, core):
    q_owned = candidates.shape[0]
    count = doc_tokens.shape[0]
    gathered = lax.all_gather(queries, INDEX_AXES, axis=0, tiled=True)
    other = lax.ppermute(doc_tokens, "dim", [(s, cores - 1 - s) for s in range(cores)])

    def put(scores, out_refs):
        out_refs[0][...] = scores

    own, other = stage(doc_lens, doc_tokens, other)
    block = score([gathered], own, other, put, [(n * q_owned, count)])[0]
    moved = lax.all_to_all(
        block.reshape(n, q_owned, count), INDEX_AXES, split_axis=0, concat_axis=0, tiled=True
    )
    table = moved.transpose(1, 0, 2).reshape(q_owned, n * count)
    return pick(candidates, [table], [0])


def per_device(queries, doc_tokens, doc_lens, candidates):
    sizes = n_z, n_x, cores = tuple(lax.axis_size(axis) for axis in ALL_AXES)
    count = doc_tokens.shape[0]
    core = lax.axis_index("dim")
    if sizes == (4, 2, 2) and count & (count - 1) == 0:
        return four_by_two(queries, doc_tokens, doc_lens, candidates, core)
    return any_columns(queries, doc_tokens, doc_lens, candidates, n_z * n_x, cores, core)


def solution(mesh):
    in_specs = (
        P(("groups",) + INDEX_AXES, None, None),
        P(("groups",) + INDEX_AXES, "dim", None),
        P(("groups",) + INDEX_AXES),
        P(("groups",) + INDEX_AXES, None),
    )
    out_specs = P(("groups",) + INDEX_AXES, None)
    return jax.shard_map(
        per_device, mesh=mesh, in_specs=in_specs, out_specs=out_specs, check_vma=False
    )
```
